128 devices in a mesh: expert: 32 (over z, x, core), opt: 4 (over y).
Axes of the slice: x: 4, y: 4, z: 4, core: 2. Of those that a mesh axis runs over, the one named last changes fastest.
Arguments:
- out_grad: bfloat16 [65536, 2048], P(('expert', 'opt')), may hold values from -6 to 6
- saved_input: bfloat16 [65536, 768], P(('expert', 'opt')), may hold values from -6 to 6
- route: int32 [65536, 1], P(('expert', 'opt')), may hold values from 0 to 127, as said below
- place_now: int32 [128], replicated, may hold values from 0 to 31, as said below
- place_next: int32 [128], replicated, may hold values from 0 to 31, as said below
- master: float32 [32, 1572864], P(None, ('expert', 'opt')), may hold values from -0.21875 to 0.21875
- moment_one: float32 [32, 1572864], P(None, ('expert', 'opt')), may hold values from -2 to 2
- moment_two: float32 [32, 1572864], P(None, ('expert', 'opt')), may hold values from 0.01 to 1
- fwd_input: bfloat16 [131072, 768], P(('expert', 'opt')), may hold values from -6 to 6
Outputs:
- input_grad: bfloat16 [65536, 768], P(('expert', 'opt'))
- new_master: float32 [32, 1572864], P(None, ('expert', 'opt'))
- new_moment_one: float32 [32, 1572864], P(None, ('expert', 'opt'))
- new_moment_two: float32 [32, 1572864], P(None, ('expert', 'opt'))
- fwd_output: bfloat16 [131072, 2048], P(('expert', 'opt'))
The draws below stay inside these ranges and needn't reach their ends.
Inputs may be any that keep to these rules, and one draw needn't show every extreme that they name: `route`: among the 512 rows of one device, at most 8 go to one replica device; in every draw some replica device receives exactly 8 rows from every device. `place_now`: every one of the 32 experts holds at least one replica slot. `place_next`: every one of the 32 experts holds at least one replica slot.
All inputs are finite; a program needn't handle non-finite values.
Results may differ from the reference program's by a relative error of at most 0.005.
Values may be sent and summed in bfloat16 or wider, within the bound.
No kernel may reach another device: no remote copies, remote signals or barrier semaphores. Data moves between devices by JAX's collectives and lax.ppermute only.
A program may use at most 128 MiB of HBM per device.

```python
import math
import jax
import jax.numpy as jnp
from jax import lax

D = 2048
FF = 768
TOK_DEV = 512
FWD_ROWS = 1024
EXPERTS = 32
CAP = 8
TOKENS = 65536
N_EXPERT = 32
N_OPT = 4
DEVICES = 128


def draw_route(key, part):
    device_count = N_EXPERT * N_OPT
    slot_count = device_count * CAP
    key_full, key_popular, key_blocks = jax.random.split(jax.random.fold_in(key, 11), 3)
    full_target = jax.random.randint(key_full, (), 0, device_count)
    popularity = jax.random.randint(key_popular, (device_count,), 0, 4)
    slot_owner = jnp.arange(slot_count, dtype=jnp.int32) // CAP

    def one_block(block_key):
        key_noise, key_shuffle = jax.random.split(block_key)
        noise_draw = jax.random.randint(key_noise, (slot_count,), 0, 1024)
        scores = (noise_draw + 512 * popularity[slot_owner]) * slot_count + jnp.arange(slot_count, dtype=jnp.int32)
        scores = jnp.where(slot_owner == full_target, jnp.int32(2 ** 30), scores)
        _, chosen_slots = lax.top_k(scores, TOK_DEV)
        chosen = slot_owner[chosen_slots]
        return jax.random.permutation(key_shuffle, chosen)
    blocks = jax.vmap(one_block)(jax.random.split(key_blocks, device_count))
    return blocks.reshape(TOK_DEV * device_count, 1).astype(jnp.int32)


def draw_placement(key, salt_value):
    device_count = N_EXPERT * N_OPT
    key_first, key_left, key_right, key_label, key_shuffle = jax.random.split(jax.random.fold_in(key, salt_value), 5)
    first_pass = jax.random.permutation(key_first, EXPERTS)
    relabel = jax.random.permutation(key_label, EXPERTS)
    extra_count = device_count - EXPERTS
    low_pick = jnp.minimum(jax.random.randint(key_left, (extra_count,), 0, EXPERTS), jax.random.randint(key_right, (extra_count,), 0, EXPERTS))
    extra_slots = relabel[low_pick]
    combined = jnp.concatenate([first_pass, extra_slots]).astype(jnp.int32)
    return jax.random.permutation(key_shuffle, combined).astype(jnp.int32)


def draw_place_now(key, part):
    return draw_placement(key, 3)


def draw_place_next(key, part):
    return draw_placement(key, 5)


def block_levels(key, shape, shards, least, high):
    level, own = 1.0, jax.random.fold_in(key, 6)
    for dim, parts in shards:
        draws = jnp.exp(jax.random.uniform(jax.random.fold_in(own, dim), (parts,), jnp.float32, least / len(shards), high / len(shards)))
        level = level * jnp.repeat(draws, shape[dim] // parts).reshape([-1 if axis == dim else 1 for axis in range(len(shape))])
    return level


def centred(rng, shape, spread, reach, cuts=(), kind=jnp.bfloat16):
    factor_of = block_levels(rng, shape, cuts, -0.22, 0.18) if cuts else 1.0
    entries = jax.random.normal(rng, shape, jnp.float32) * spread * factor_of
    return jnp.minimum(jnp.maximum(entries, -reach), reach).astype(kind)


def setup_inputs(seed: int = 0) -> dict:
    key_of = jax.random.split(jax.random.key(seed), 10)
    out_grad = centred(key_of[0], (TOKENS, D), 1.0, 6.0, ((0, 128),))
    saved_input = centred(key_of[1], (TOKENS, FF), 1.0, 6.0, ((0, 128),))
    route = draw_route(jax.random.fold_in(key_of[9], 71), 0)
    place_now = draw_place_now(jax.random.fold_in(key_of[9], 71), 0)
    place_next = draw_place_next(jax.random.fold_in(key_of[9], 71), 0)
    master = centred(key_of[5], (EXPERTS, FF * D), FF ** -0.5, 0.21875, ((1, 128),), jnp.float32)
    moment_one = centred(key_of[6], (EXPERTS, FF * D), 0.3, 2.0, ((1, 128),), jnp.float32)
    moment_two = jnp.clip(jnp.exp(math.log(1.0) - 4.6051702 * jax.random.uniform(key_of[7], (EXPERTS, FF * D), jnp.float32) ** block_levels(key_of[7], (EXPERTS, FF * D), ((1, 128),), -0.2, 0.2)), 0.01, 1.0)
    fwd_input = centred(key_of[8], (DEVICES * FWD_ROWS, FF), 1.0, 6.0, ((0, 128),))
    return dict(out_grad=out_grad, saved_input=saved_input, route=route, place_now=place_now, place_next=place_next, master=master, moment_one=moment_one, moment_two=moment_two, fwd_input=fwd_input)


LOSS_SCALE = 64.0
BETA_ONE = 0.9
BETA_TWO = 0.95
LEARN_RATE = 0.002
DECAY = 0.1
EPSILON = 1e-08
STEP_COUNT = 20.0

def reference(out_grad, saved_input, route, place_now, place_next, master, moment_one, moment_two, fwd_input):
    device_count = N_EXPERT * N_OPT
    window = device_count * CAP
    target = route[:, 0].astype(jnp.int32)
    sorted_order = jnp.argsort(target, stable=True).astype(jnp.int32)
    counts = lax.optimization_barrier(jnp.sum((target[:, None] == jnp.arange(device_count, dtype=jnp.int32)[None, :]).astype(jnp.int32), axis=0))
    starts = (jnp.cumsum(counts) - counts).astype(jnp.int32)
    grad_pad = jnp.concatenate([out_grad[sorted_order], jnp.zeros((window, D), out_grad.dtype)], axis=0)
    hidden_pad = jnp.concatenate([saved_input[sorted_order], jnp.zeros((window, FF), saved_input.dtype)], axis=0)
    weights_now = master.astype(jnp.bfloat16)

    def visit_replica(state_pair, replica):
        gradient_sum, input_sorted = state_pair
        start = starts[replica]
        live_mask = (jnp.arange(window, dtype=jnp.int32) < counts[replica])[:, None]
        grad_rows = lax.dynamic_slice_in_dim(grad_pad, start, window, 0)
        hidden_rows = lax.dynamic_slice_in_dim(hidden_pad, start, window, 0)
        grad_rows = jnp.where(live_mask, grad_rows, jnp.zeros_like(grad_rows))
        hidden_rows = jnp.where(live_mask, hidden_rows, jnp.zeros_like(hidden_rows))
        expert = place_now[replica]
        weight_now = lax.dynamic_index_in_dim(weights_now, expert, 0, keepdims=False).reshape(FF, D)
        partial_value = lax.dot_general(hidden_rows, grad_rows, (((0,), (0,)), ((), ())), preferred_element_type=jnp.float32)
        partial_wire = lax.optimization_barrier((partial_value / LOSS_SCALE).astype(jnp.bfloat16))
        gradient_sum = gradient_sum.at[expert].add(partial_wire.astype(jnp.float32).reshape(-1))
        input_part = lax.dot_general(grad_rows, weight_now, (((1,), (1,)), ((), ())), preferred_element_type=jnp.float32).astype(jnp.bfloat16)
        previous = lax.dynamic_slice_in_dim(input_sorted, start, window, 0)
        input_sorted = lax.dynamic_update_slice_in_dim(input_sorted, jnp.where(live_mask, input_part, previous), start, 0)
        return ((gradient_sum, input_sorted), None)
    initial = (jnp.zeros((EXPERTS, FF * D), jnp.float32), jnp.zeros((TOKENS + window, FF), jnp.bfloat16))
    (gradient, input_sorted), _ = lax.scan(visit_replica, initial, jnp.arange(device_count, dtype=jnp.int32))
    input_grad = jnp.zeros((TOKENS, FF), jnp.bfloat16).at[sorted_order].set(input_sorted[:TOKENS])
    new_moment_one = BETA_ONE * moment_one + (1.0 - BETA_ONE) * gradient
    new_moment_two = BETA_TWO * moment_two + (1.0 - BETA_TWO) * gradient * gradient
    first_hat = new_moment_one / (1.0 - BETA_ONE ** STEP_COUNT)
    second_hat = new_moment_two / (1.0 - BETA_TWO ** STEP_COUNT)
    new_master = master - LEARN_RATE * (first_hat / (jnp.sqrt(second_hat) + EPSILON) + DECAY * master)
    weights_next = new_master.astype(jnp.bfloat16)
    blocks = fwd_input.reshape(device_count, FWD_ROWS, FF)

    def forward_block(pair):
        rows_block, expert = pair
        weight_next = lax.dynamic_index_in_dim(weights_next, expert, 0, keepdims=False).reshape(FF, D)
        return jnp.dot(rows_block, weight_next, preferred_element_type=jnp.float32).astype(jnp.bfloat16)
    fwd_output = lax.map(forward_block, (blocks, place_next)).reshape(device_count * FWD_ROWS, D)
    return (input_grad, new_master, new_moment_one, new_moment_two, fwd_output)
```

```python
import functools

import jax
import jax.numpy as jnp
from jax import lax
from jax.experimental import pallas as pl
from jax.experimental.pallas import tpu as pltpu
from jax.sharding import PartitionSpec as P

LOSS_SCALE = 64.0
BETA_ONE = 0.9
BETA_TWO = 0.95
LEARN_RATE = 0.002
DECAY = 0.1
EPSILON = 1e-08
STEP_COUNT = 20.0

D = 2048
FF = 768
ROWS = 512
FWD_ROWS = 1024
EXPERTS = 32
DEVICES = 128
CAP = 8
SLOTS = DEVICES * CAP
OWN = FF // DEVICES
BLOCK = OWN * D // 8
HALVES = D // 1024
SEND_ONE = FF + D + BLOCK
SEND_TWO = FF + BLOCK
LANES = 256
MIB = 1 << 20

BF16 = jnp.bfloat16
F32 = jnp.float32
I32 = jnp.int32


def iota(shape, dim):
    return lax.broadcasted_iota(I32, shape, dim)


def mm(a, b, dims=((1,), (0,))):
    return lax.dot_general(a, b, (dims, ((), ())), preferred_element_type=F32)


def pick_rows(place_row):
    shape = (SLOTS, DEVICES)
    spread = jnp.where(iota(shape, 0) // 8 == iota(shape, 1), place_row, 0)
    mine = jnp.sum(spread.astype(F32), axis=1, keepdims=True).astype(I32)
    shape = (SLOTS, 8 * EXPERTS)
    row, col = iota(shape, 0), iota(shape, 1)
    hit = (col % EXPERTS == mine) & (col // EXPERTS == row % 8)
    return jnp.where(hit, 1.0, 0.0).astype(BF16)


def pick_columns(place_row):
    shape = (DEVICES, SLOTS)
    wide = jnp.where(iota(shape, 1) // 8 == iota(shape, 0), 1.0, 0.0).astype(BF16)
    mine = mm(place_row.astype(F32).astype(BF16), wide).astype(I32)
    shape = (8 * EXPERTS, SLOTS)
    row, col = iota(shape, 0), iota(shape, 1)
    hit = (row % EXPERTS == mine) & (row // EXPERTS == col % 8)
    return jnp.where(hit, 1.0, 0.0).astype(BF16)


def block_order(to_blocks):
    size = 8 * 8 * OWN
    shape = (size, size)
    blk, mat = (iota(shape, 0), iota(shape, 1)) if to_blocks else (iota(shape, 1), iota(shape, 0))
    target = (blk % 8) * (8 * OWN) + (blk // 8 % 8) * OWN + blk // 64
    return jnp.where(target == mat, 1.0, 0.0).astype(BF16)


def matrix_from_blocks(parts, weight, perm):
    for g in range(DEVICES // 8):
        rows = pl.ds(g * 64, 64)
        stacked = jnp.concatenate([p[rows, :] for p in parts], axis=0)
        moved = mm(perm, stacked).astype(BF16)
        for s in range(8):
            for h in range(HALVES):
                weight[pl.ds(g * 8 * OWN, 8 * OWN), pl.ds((h * 8 + s) * 128, 128)] = moved[
                    s * 8 * OWN : (s + 1) * 8 * OWN, h * 128 : (h + 1) * 128
                ]


def stacked_master(block):
    return jnp.concatenate(
        [
            jnp.concatenate(
                [block[:, (h * 8 + s) * 128 : (h * 8 + s + 1) * 128] for h in range(HALVES)], axis=1
            )
            for s in range(8)
        ],
        axis=0,
    )


def dispatch_kernel(route, place, saved, grad, master, send, position, slot_of, pick):
    j = pl.program_id(0)

    @pl.when(j == 0)
    def _():
        target = route[...]
        hits = iota((DEVICES, ROWS), 0) == target
        ones = jnp.where(hits, 1.0, 0.0)
        shape = (ROWS, ROWS)
        upto = jnp.where(iota(shape, 0) < iota(shape, 1), 1.0, 0.0).astype(BF16)
        earlier = mm(ones.astype(BF16), upto)
        rank = jnp.sum(ones * earlier, axis=0, keepdims=True).astype(I32)
        where = target * CAP + rank
        position[...] = where
        slot_of[...] = jnp.where(iota((SLOTS, ROWS), 0) == where, 1.0, 0.0).astype(BF16)
        pick[...] = pick_rows(place[...])

    @pl.when(j < 3)
    def _():
        send[...] = mm(slot_of[...], saved[...]).astype(BF16)

    @pl.when((j >= 3) & (j < 11))
    def _():
        send[...] = mm(slot_of[...], grad[...]).astype(BF16)

    @pl.when(j >= 11)
    def _():
        send[...] = mm(pick[...], stacked_master(master[...]).astype(BF16)).astype(BF16)


def dispatch(route, place, saved, grad, master):
    return pl.pallas_call(
        dispatch_kernel,
        grid=(SEND_ONE // LANES,),
        in_specs=[
            pl.BlockSpec((1, ROWS), lambda j: (0, 0)),
            pl.BlockSpec((1, DEVICES), lambda j: (0, 0)),
            pl.BlockSpec((ROWS, LANES), lambda j: (0, jnp.minimum(j, 2))),
            pl.BlockSpec((ROWS, LANES), lambda j: (0, jnp.clip(j - 3, 0, 7))),
            pl.BlockSpec((EXPERTS, D), lambda j: (0, jnp.clip(j - 11, 0, 5))),
        ],
        out_specs=[
            pl.BlockSpec((SLOTS, LANES), lambda j: (0, j)),
            pl.BlockSpec((1, ROWS), lambda j: (0, 0)),
        ],
        out_shape=[
            jax.ShapeDtypeStruct((SLOTS, SEND_ONE), BF16),
            jax.ShapeDtypeStruct((1, ROWS), I32),
        ],
        scratch_shapes=[pltpu.VMEM((SLOTS, ROWS), BF16), pltpu.VMEM((SLOTS, 8 * EXPERTS), BF16)],
        compiler_params=pltpu.CompilerParams(vmem_limit_bytes=32 * MIB),
        cost_estimate=pl.CostEstimate(flops=4_000_000_000, bytes_accessed=14_000_000, transcendentals=0),
        name="dispatch_rows",
    )(route, place, saved, grad, master)


def partial_kernel(hidden, *refs):
    grads, out = refs[:8], refs[8]
    perm = block_order(True)
    left = hidden[...].T
    pieces = [(mm(left, g[...]) * (1.0 / LOSS_SCALE)).astype(BF16) for g in grads]
    chunks = [p[:, c * 128 : (c + 1) * 128] for p in pieces for c in range(2)]
    for g in range(FF // 2 // (8 * OWN)):
        rows = slice(g * 8 * OWN, (g + 1) * 8 * OWN)
        stacked = jnp.concatenate(
            [
                jnp.concatenate([chunks[h * 8 + s][rows, :] for h in range(HALVES)], axis=1)
                for s in range(8)
            ],
            axis=0,
        )
        moved = mm(perm, stacked).astype(BF16)
        for f in range(OWN):
            out[pl.ds(g * 64, 64), pl.ds(f * LANES, LANES)] = moved[f * 64 : (f + 1) * 64, :]


def grad_spec(rows, k, index):
    return pl.BlockSpec((rows, LANES), lambda m: (index(m), 3 + k))


def partials(got):
    return pl.pallas_call(
        partial_kernel,
        grid=(2,),
        in_specs=[pl.BlockSpec((SLOTS, FF // 2), lambda m: (0, m))]
        + [grad_spec(SLOTS, k, lambda m: 0) for k in range(8)],
        out_specs=pl.BlockSpec((SLOTS // 2, BLOCK), lambda m: (m, 0)),
        out_shape=jax.ShapeDtypeStruct((SLOTS, BLOCK), BF16),
        compiler_params=pltpu.CompilerParams(vmem_limit_bytes=48 * MIB),
        cost_estimate=pl.CostEstimate(flops=4_400_000_000, bytes_accessed=9_000_000, transcendentals=0),
        name="partial_blocks",
    )(*([got] * 9))


def input_kernel(position, place_now, place_next, *refs):
    parts, grads = refs[:OWN], refs[OWN : OWN + 8]
    out, back, sum_now, pick_next, weight = refs[OWN + 8 :]

    @pl.when(pl.program_id(0) == 0)
    def _():
        matrix_from_blocks(parts, weight, block_order(False))
        shape = (ROWS, ROWS)
        spread = jnp.where(iota(shape, 0) == iota(shape, 1), position[...], 0)
        where = jnp.sum(spread.astype(F32), axis=1, keepdims=True).astype(I32)
        back[...] = jnp.where(iota((ROWS, SLOTS), 1) == where, 1.0, 0.0).astype(BF16)
        sum_now[...] = pick_columns(place_now[...])
        pick_next[...] = pick_rows(place_next[...])

    rows = jnp.concatenate([g[...] for g in grads], axis=1)
    out[...] = mm(rows, weight[...], ((1,), (1,))).astype(BF16)


def input_parts(got, position, place_now, place_next):
    tall = 256
    return pl.pallas_call(
        input_kernel,
        grid=(SLOTS // tall,),
        in_specs=[
            pl.BlockSpec((1, ROWS), lambda m: (0, 0)),
            pl.BlockSpec((1, DEVICES), lambda m: (0, 0)),
            pl.BlockSpec((1, DEVICES), lambda m: (0, 0)),
        ]
        + [pl.BlockSpec((SLOTS, LANES), functools.partial(lambda f, m: (0, 11 + f), f)) for f in range(OWN)]
        + [grad_spec(tall, k, lambda m: m) for k in range(8)],
        out_specs=[
            pl.BlockSpec((tall, FF), lambda m: (m, 0)),
            pl.BlockSpec((ROWS, SLOTS), lambda m: (0, 0)),
            pl.BlockSpec((8 * EXPERTS, SLOTS), lambda m: (0, 0)),
            pl.BlockSpec((SLOTS, 8 * EXPERTS), lambda m: (0, 0)),
        ],
        out_shape=[
            jax.ShapeDtypeStruct((SLOTS, SEND_TWO), BF16),
            jax.ShapeDtypeStruct((ROWS, SLOTS), BF16),
            jax.ShapeDtypeStruct((8 * EXPERTS, SLOTS), BF16),
            jax.ShapeDtypeStruct((SLOTS, 8 * EXPERTS), BF16),
        ],
        scratch_shapes=[pltpu.VMEM((FF, D), BF16)],
        compiler_params=pltpu.CompilerParams(vmem_limit_bytes=48 * MIB),
        cost_estimate=pl.CostEstimate(flops=4_400_000_000, bytes_accessed=12_000_000, transcendentals=0),
        name="input_parts",
    )(position, place_now, place_next, *([got] * (OWN + 8)))


def adam_kernel(sum_now, pick_next, arrived, master, one, two, _, send, new_master, new_one, new_two):
    total = mm(sum_now[...], arrived[...])
    rows = []
    for s in range(8):
        across = []
        for h in range(HALVES):
            gradient = total[s * EXPERTS : (s + 1) * EXPERTS, h * 128 : (h + 1) * 128]
            at = pl.ds((h * 8 + s) * 128, 128)
            weight = master[:, at]
            first = BETA_ONE * one[:, at] + (1.0 - BETA_ONE) * gradient
            second = BETA_TWO * two[:, at] + (1.0 - BETA_TWO) * gradient * gradient
            first_hat = first * (1.0 / (1.0 - BETA_ONE**STEP_COUNT))
            second_hat = second * (1.0 / (1.0 - BETA_TWO**STEP_COUNT))
            updated = weight - LEARN_RATE * (first_hat / (jnp.sqrt(second_hat) + EPSILON) + DECAY * weight)
            new_one[:, at] = first
            new_two[:, at] = second
            new_master[:, at] = updated
            across.append(updated.astype(BF16))
        rows.append(jnp.concatenate(across, axis=1))
    send[...] = mm(pick_next[...], jnp.concatenate(rows, axis=0)).astype(BF16)


def adam(sum_now, pick_next, arrived, master, one, two, send):
    owned = pl.BlockSpec((EXPERTS, D), lambda f: (0, f))
    state = jax.ShapeDtypeStruct(master.shape, F32)
    return pl.pallas_call(
        adam_kernel,
        grid=(OWN,),
        in_specs=[
            pl.BlockSpec((8 * EXPERTS, SLOTS), lambda f: (0, 0)),
            pl.BlockSpec((SLOTS, 8 * EXPERTS), lambda f: (0, 0)),
            pl.BlockSpec((SLOTS, LANES), lambda f: (0, f)),
            owned,
            owned,
            owned,
            pl.BlockSpec(memory_space=pl.ANY),
        ],
        out_specs=[pl.BlockSpec((SLOTS, LANES), lambda f: (0, 3 + f)), owned, owned, owned],
        out_shape=[jax.ShapeDtypeStruct((SLOTS, SEND_TWO), BF16), state, state, state],
        input_output_aliases={6: 0},
        compiler_params=pltpu.CompilerParams(vmem_limit_bytes=32 * MIB),
        cost_estimate=pl.CostEstimate(flops=1_700_000_000, bytes_accessed=16_000_000, transcendentals=400_000),
        name="adam_step",
    )(sum_now, pick_next, arrived, master, one, two, send)


def forward_kernel(*refs):
    parts, (returned, back, rows, out, input_grad, weight) = refs[:OWN], refs[OWN:]
    m = pl.program_id(0)

    @pl.when(m == 0)
    def _():
        matrix_from_blocks(parts, weight, block_order(False))

    out[...] = mm(rows[...], weight[...]).astype(BF16)
    input_grad[...] = mm(back[...], returned[...]).astype(BF16)


def forward(landed, back, rows):
    steps = 4
    tall = FWD_ROWS // steps
    return pl.pallas_call(
        forward_kernel,
        grid=(steps,),
        in_specs=[
            pl.BlockSpec((SLOTS, LANES), functools.partial(lambda f, m: (0, 3 + f), f)) for f in range(OWN)
        ]
        + [
            pl.BlockSpec((SLOTS, FF), lambda m: (0, 0)),
            pl.BlockSpec((ROWS // steps, SLOTS), lambda m: (m, 0)),
            pl.BlockSpec((tall, FF), lambda m: (m, 0)),
        ],
        out_specs=[
            pl.BlockSpec((tall, D), lambda m: (m, 0)),
            pl.BlockSpec((ROWS // steps, FF), lambda m: (m, 0)),
        ],
        out_shape=[
            jax.ShapeDtypeStruct((FWD_ROWS, D), BF16),
            jax.ShapeDtypeStruct((ROWS, FF), BF16),
        ],
        scratch_shapes=[pltpu.VMEM((FF, D), BF16)],
        compiler_params=pltpu.CompilerParams(vmem_limit_bytes=48 * MIB),
        cost_estimate=pl.CostEstimate(flops=5_200_000_000, bytes_accessed=13_000_000, transcendentals=0),
        name="forward_rows",
    )(*([landed] * (OWN + 1)), back, rows)


def exchange(blocks):
    split = blocks.reshape(DEVICES, 8, blocks.shape[1])
    moved = lax.all_to_all(split, ("expert", "opt"), split_axis=0, concat_axis=0, tiled=True)
    return moved.reshape(blocks.shape)


def per_device(out_grad, saved_input, route, place_now, place_next, master, moment_one, moment_two, fwd_input):
    now, then = place_now.reshape(1, DEVICES), place_next.reshape(1, DEVICES)
    send, position = dispatch(route.reshape(1, ROWS), now, saved_input, out_grad, master)
    got = exchange(send)
    arrived = exchange(partials(got))
    sending, back, sum_now, pick_next = input_parts(got, position, now, then)
    sending, new_master, new_one, new_two = adam(
        sum_now, pick_next, arrived, master, moment_one, moment_two, sending
    )
    landed = exchange(sending)
    fwd_output, input_grad = forward(landed, back, fwd_input)
    return (input_grad, new_master, new_one, new_two, fwd_output)


def solution(mesh):
    split_rows = P(("expert", "opt"), None)
    split_columns = P(None, ("expert", "opt"))
    return jax.shard_map(
        per_device,
        mesh=mesh,
        in_specs=(split_rows, split_rows, split_rows, P(), P())
        + (split_columns, split_columns, split_columns, split_rows),
        out_specs=(split_rows, split_columns, split_columns, split_columns, split_rows),
        check_vma=False,
    )
```

```python
import jax
import jax.numpy as jnp
from jax import lax
from jax.experimental import pallas as pl
from jax.experimental.pallas import tpu as pltpu
from jax.sharding import PartitionSpec as P

LOSS_SCALE = 64.0
BETA_ONE = 0.9
BETA_TWO = 0.95
LEARN_RATE = 0.002
DECAY = 0.1
EPSILON = 1e-08
STEP_COUNT = 20.0

D = 2048
FF = 768
ROWS = 512
FWD_ROWS = 1024
EXPERTS = 32
DEVICES = 128
CAP = 8
SLOTS = DEVICES * CAP
OWN = FF // DEVICES
BLOCK = OWN * D // 8
HALVES = D // 1024
SEND_ONE = FF + D + BLOCK
SEND_TWO = FF + BLOCK
LANES = 256
MIB = 1 << 20

BF16 = jnp.bfloat16
F32 = jnp.float32
I32 = jnp.int32


def iota(shape, dim):
    return lax.broadcasted_iota(I32, shape, dim)


def mm(a, b, dims=((1,), (0,))):
    return lax.dot_general(a, b, (dims, ((), ())), preferred_element_type=F32)


def pick_rows(place_row):
    shape = (SLOTS, DEVICES)
    spread = jnp.where(iota(shape, 0) // 8 == iota(shape, 1), place_row, 0)
    mine = jnp.sum(spread.astype(F32), axis=1, keepdims=True).astype(I32)
    shape = (SLOTS, 8 * EXPERTS)
    row, col = iota(shape, 0), iota(shape, 1)
    hit = (col % EXPERTS == mine) & (col // EXPERTS == row % 8)
    return jnp.where(hit, 1.0, 0.0).astype(BF16)


def pick_columns(place_row):
    shape = (DEVICES, SLOTS)
    wide = jnp.where(iota(shape, 1) // 8 == iota(shape, 0), 1.0, 0.0).astype(BF16)
    mine = mm(place_row.astype(F32).astype(BF16), wide).astype(I32)
    shape = (8 * EXPERTS, SLOTS)
    row, col = iota(shape, 0), iota(shape, 1)
    hit = (row % EXPERTS == mine) & (row // EXPERTS == col % 8)
    return jnp.where(hit, 1.0, 0.0).astype(BF16)


def block_order(to_blocks):
    size = 8 * 8 * OWN
    shape = (size, size)
    blk, mat = (iota(shape, 0), iota(shape, 1)) if to_blocks else (iota(shape, 1), iota(shape, 0))
    target = (blk % 8) * (8 * OWN) + (blk // 8 % 8) * OWN + blk // 64
    return jnp.where(target == mat, 1.0, 0.0).astype(BF16)


def copies(pairs, sems, first=0):
    made = [pltpu.make_async_copy(a, b, sems.at[first + k]) for k, (a, b) in enumerate(pairs)]
    for copy in made:
        copy.start()
    return made


def lanes(k, width=LANES):
    return pl.ds(k * width, width)


NEAR, FAR = pltpu.VMEM, pltpu.HBM


def call(kernel, ins, outs, scratch, mib, flops, moved, name, **more):
    near = pl.BlockSpec(memory_space=NEAR)
    far = pl.BlockSpec(memory_space=pl.ANY)
    run = pl.pallas_call(
        kernel,
        in_specs=[near if space is NEAR else far for _, space in ins],
        out_specs=[near if space is NEAR else far for space, _, _ in outs],
        out_shape=[space(shape, kind) for space, shape, kind in outs],
        scratch_shapes=scratch,
        compiler_params=pltpu.CompilerParams(vmem_limit_bytes=mib * MIB),
        cost_estimate=pl.CostEstimate(flops=flops, bytes_accessed=moved, transcendentals=0),
        name=name,
        **more,
    )
    return run(*[pltpu.with_memory_space_constraint(x, space) for x, space in ins])


def matrix_half(blocks, start, weight, perm, h):
    for pair in range(DEVICES // 16):
        stacked = jnp.concatenate(
            [
                jnp.concatenate(
                    [
                        blocks[pl.ds((pair * 2 + g) * 64, 64), pl.ds(start + (f * HALVES + h) * 128, 128)]
                        for g in range(2)
                    ],
                    axis=1,
                )
                for f in range(OWN)
            ],
            axis=0,
        )
        moved = mm(perm, stacked).astype(BF16)
        for g in range(2):
            for s in range(8):
                weight[pl.ds((pair * 2 + g) * 8 * OWN, 8 * OWN), pl.ds((h * 8 + s) * 128, 128)] = moved[
                    s * 8 * OWN : (s + 1) * 8 * OWN, g * 128 : (g + 1) * 128
                ]


def blocks_half(matrix, blocks, perm, h):
    for pair in range(DEVICES // 16):
        stacked = jnp.concatenate(
            [
                jnp.concatenate(
                    [
                        matrix[pl.ds((pair * 2 + g) * 8 * OWN, 8 * OWN), pl.ds((h * 8 + s) * 128, 128)]
                        for g in range(2)
                    ],
                    axis=1,
                )
                for s in range(8)
            ],
            axis=0,
        )
        moved = mm(perm, stacked).astype(BF16)
        for g in range(2):
            for f in range(OWN):
                blocks[pl.ds((pair * 2 + g) * 64, 64), pl.ds((f * HALVES + h) * 128, 128)] = moved[
                    f * 64 : (f + 1) * 64, g * 128 : (g + 1) * 128
                ]


def stacked_master(block):
    return jnp.concatenate(
        [
            jnp.concatenate(
                [block[:, (h * 8 + s) * 128 : (h * 8 + s + 1) * 128] for h in range(HALVES)], axis=1
            )
            for s in range(8)
        ],
        axis=0,
    )


def dispatch_kernel(
    route, place, saved, grad, master, send, position, route_v, place_v, saved_v, grad_v, master_v, position_v, sems
):
    got_route, got_place, got_saved, got_grad, got_master = copies(
        [(route, route_v), (place, place_v), (saved, saved_v), (grad, grad_v), (master, master_v)], sems
    )
    got_route.wait()
    target = route_v[...]
    ones = jnp.where(iota((DEVICES, ROWS), 0) == target, 1.0, 0.0)
    shape = (ROWS, ROWS)
    upto = jnp.where(iota(shape, 0) < iota(shape, 1), 1.0, 0.0).astype(BF16)
    earlier = mm(ones.astype(BF16), upto)
    rank = jnp.sum(ones * earlier, axis=0, keepdims=True).astype(I32)
    where = target * CAP + rank
    position_v[...] = where
    (told,) = copies([(position_v, position)], sems, 5)
    slot_of = jnp.where(iota((SLOTS, ROWS), 0) == where, 1.0, 0.0).astype(BF16)
    got_place.wait()
    pick = pick_rows(place_v[...])
    got_saved.wait()
    for k in range(3):
        send[:, lanes(k)] = mm(slot_of, saved_v[:, lanes(k)]).astype(BF16)
    got_grad.wait()
    for k in range(8):
        send[:, lanes(3 + k)] = mm(slot_of, grad_v[:, lanes(k)]).astype(BF16)
    got_master.wait()
    for f in range(OWN):
        rows = stacked_master(master_v[:, lanes(f, D)]).astype(BF16)
        send[:, lanes(11 + f)] = mm(pick, rows).astype(BF16)
    told.wait()


def dispatch(route, place, saved, grad, master):
    return call(
        dispatch_kernel,
        [(route, FAR), (place, FAR), (saved, FAR), (grad, FAR), (master, FAR)],
        [(NEAR, (SLOTS, SEND_ONE), BF16), (FAR, (1, ROWS), I32)],
        [
            pltpu.VMEM((1, ROWS), I32),
            pltpu.VMEM((1, DEVICES), I32),
            pltpu.VMEM((ROWS, FF), BF16),
            pltpu.VMEM((ROWS, D), BF16),
            pltpu.VMEM((EXPERTS, OWN * D), F32),
            pltpu.VMEM((1, ROWS), I32),
            pltpu.SemaphoreType.DMA((6,)),
        ],
        16,
        4_000_000_000,
        14_000_000,
        "dispatch_rows",
    )


def partial_kernel(got, out, part_v, out_v, sems):
    perm = block_order(True)
    left = got[:, pl.ds(0, FF)].T
    sent = []
    for h in range(HALVES):
        for k in range(4 * h, 4 * h + 4):
            part_v[:, lanes(k)] = (mm(left, got[:, lanes(3 + k)]) * (1.0 / LOSS_SCALE)).astype(BF16)
        blocks_half(part_v, out_v, perm, h)
        for f in range(OWN):
            at = lanes(f * HALVES + h, 128)
            sent += copies([(out_v.at[:, at], out.at[:, at])], sems, h * OWN + f)
    for copy in sent:
        copy.wait()


def partials(got):
    return call(
        partial_kernel,
        [(got, NEAR)],
        [(FAR, (SLOTS, BLOCK), BF16)],
        [
            pltpu.VMEM((FF, D), BF16),
            pltpu.VMEM((SLOTS, BLOCK), BF16),
            pltpu.SemaphoreType.DMA((HALVES * OWN,)),
        ],
        20,
        4_400_000_000,
        9_000_000,
        "partial_blocks",
    )[0]


def input_kernel(position, got, out, back, position_v, weight, out_v, back_v, sems):
    (got_position,) = copies([(position, position_v)], sems)
    perm = block_order(False)
    for h in range(HALVES):
        matrix_half(got, FF + D, weight, perm, h)
    sent = []
    for k in range(4):
        rows = pl.ds(k * 256, 256)
        out_v[rows, :] = mm(got[rows, pl.ds(FF, D)], weight[...], ((1,), (1,))).astype(BF16)
        sent += copies([(out_v.at[rows, :], out.at[rows, :])], sems, 1 + k)
    got_position.wait()
    shape = (ROWS, ROWS)
    spread = jnp.where(iota(shape, 0) == iota(shape, 1), position_v[...], 0)
    where = jnp.sum(spread.astype(F32), axis=1, keepdims=True).astype(I32)
    back_v[...] = jnp.where(iota((ROWS, SLOTS), 1) == where, 1.0, 0.0).astype(BF16)
    sent += copies([(back_v, back)], sems, 5)
    for copy in sent:
        copy.wait()


def input_parts(got, position):
    return call(
        input_kernel,
        [(position, FAR), (got, NEAR)],
        [(FAR, (SLOTS, FF), BF16), (FAR, (ROWS, SLOTS), BF16)],
        [
            pltpu.VMEM((1, ROWS), I32),
            pltpu.VMEM((FF, D), BF16),
            pltpu.VMEM((SLOTS, FF), BF16),
            pltpu.VMEM((ROWS, SLOTS), BF16),
            pltpu.SemaphoreType.DMA((6,)),
        ],
        20,
        4_400_000_000,
        12_000_000,
        "input_parts",
    )


def adam_kernel(
    place_now, place_next, arrived, returning, master, one, two, send, new_master, new_one, new_two,
    now_v, then_v, master_v, one_v, two_v, next_v, first_v, second_v, place_sems, in_sems, out_sems,
):
    got_now, got_then = copies([(place_now, now_v), (place_next, then_v)], place_sems)
    landed = []
    for f in range(OWN):
        landed += copies(
            [(a.at[:, lanes(f, D)], b.at[:, lanes(f, D)]) for a, b in ((master, master_v), (one, one_v), (two, two_v))],
            in_sems,
            3 * f,
        )
    (merged,) = copies([(returning, send.at[:, pl.ds(0, FF)])], place_sems, 2)
    got_now.wait()
    sum_now = pick_columns(now_v[...])
    got_then.wait()
    pick_next = pick_rows(then_v[...])
    sent = []
    for f in range(OWN):
        total = mm(sum_now, arrived[:, lanes(f)])
        for copy in landed[3 * f : 3 * f + 3]:
            copy.wait()
        rows = []
        for s in range(8):
            across = []
            for h in range(HALVES):
                gradient = total[s * EXPERTS : (s + 1) * EXPERTS, h * 128 : (h + 1) * 128]
                at = pl.ds(f * D + (h * 8 + s) * 128, 128)
                weight = master_v[:, at]
                first = BETA_ONE * one_v[:, at] + (1.0 - BETA_ONE) * gradient
                second = BETA_TWO * two_v[:, at] + (1.0 - BETA_TWO) * gradient * gradient
                first_hat = first * (1.0 / (1.0 - BETA_ONE**STEP_COUNT))
                second_hat = second * (1.0 / (1.0 - BETA_TWO**STEP_COUNT))
                updated = weight - LEARN_RATE * (first_hat / (jnp.sqrt(second_hat) + EPSILON) + DECAY * weight)
                first_v[:, at] = first
                second_v[:, at] = second
                next_v[:, at] = updated
                across.append(updated.astype(BF16))
            rows.append(jnp.concatenate(across, axis=1))
        send[:, pl.ds(FF + f * LANES, LANES)] = mm(pick_next, jnp.concatenate(rows, axis=0)).astype(BF16)
        sent += copies(
            [
                (a.at[:, lanes(f, D)], b.at[:, lanes(f, D)])
                for a, b in ((next_v, new_master), (first_v, new_one), (second_v, new_two))
            ],
            out_sems,
            3 * f,
        )
    for copy in [merged] + sent:
        copy.wait()


def adam(place_now, place_next, arrived, returning, master, one, two):
    state = (FAR, master.shape, F32)
    flat = pltpu.VMEM((EXPERTS, OWN * D), F32)
    return call(
        adam_kernel,
        [(x, NEAR if x is arrived else FAR) for x in (place_now, place_next, arrived, returning, master, one, two)],
        [(NEAR, (SLOTS, SEND_TWO), BF16), state, state, state],
        [pltpu.VMEM((1, DEVICES), I32)] * 2
        + [flat] * 6
        + [pltpu.SemaphoreType.DMA((3,))]
        + [pltpu.SemaphoreType.DMA((3 * OWN,))] * 2,
        24,
        1_700_000_000,
        16_000_000,
        "adam_step",
    )


def forward_kernel(landed, back, rows, out, input_grad, back_v, rows_v, weight, out_v, grad_v, sems):
    got_rows, got_back = copies([(rows, rows_v), (back, back_v)], sems)
    perm = block_order(False)
    sent = []
    for h in range(HALVES):
        matrix_half(landed, FF, weight, perm, h)
        if h == 0:
            got_rows.wait()
        for k in range(4 * h, 4 * h + 4):
            out_v[:, lanes(k)] = mm(rows_v[...], weight[:, lanes(k)]).astype(BF16)
            sent += copies([(out_v.at[:, lanes(k)], out.at[:, lanes(k)])], sems, 3 + k)
        if h == 0:
            got_back.wait()
            grad_v[...] = mm(back_v[...], landed[:, pl.ds(0, FF)]).astype(BF16)
            sent += copies([(grad_v, input_grad)], sems, 2)
    for copy in sent:
        copy.wait()


def forward(landed, back, rows):
    return call(
        forward_kernel,
        [(landed, NEAR), (back, FAR), (rows, FAR)],
        [(FAR, (FWD_ROWS, D), BF16), (FAR, (ROWS, FF), BF16)],
        [
            pltpu.VMEM((ROWS, SLOTS), BF16),
            pltpu.VMEM((FWD_ROWS, FF), BF16),
            pltpu.VMEM((FF, D), BF16),
            pltpu.VMEM((FWD_ROWS, D), BF16),
            pltpu.VMEM((ROWS, FF), BF16),
            pltpu.SemaphoreType.DMA((11,)),
        ],
        24,
        5_200_000_000,
        13_000_000,
        "forward_rows",
    )


def exchange(blocks):
    split = blocks.reshape(DEVICES, 8, blocks.shape[1])
    moved = lax.all_to_all(split, ("expert", "opt"), split_axis=0, concat_axis=0, tiled=True)
    return moved.reshape(blocks.shape)


def per_device(out_grad, saved_input, route, place_now, place_next, master, moment_one, moment_two, fwd_input):
    now, then = place_now.reshape(1, DEVICES), place_next.reshape(1, DEVICES)
    send, position = dispatch(route.reshape(1, ROWS), now, saved_input, out_grad, master)
    got = exchange(send)
    arrived = exchange(partials(got))
    returning, back = input_parts(got, position)
    sending, new_master, new_one, new_two = adam(
        now, then, arrived, returning, master, moment_one, moment_two
    )
    landed = exchange(sending)
    fwd_output, input_grad = forward(landed, back, fwd_input)
    return (input_grad, new_master, new_one, new_two, fwd_output)


def solution(mesh):
    split_rows = P(("expert", "opt"), None)
    split_columns = P(None, ("expert", "opt"))
    return jax.shard_map(
        per_device,
        mesh=mesh,
        in_specs=(split_rows, split_rows, split_rows, P(), P())
        + (split_columns, split_columns, split_columns, split_rows),
        out_specs=(split_rows, split_columns, split_columns, split_columns, split_rows),
        check_vma=False,
    )
```

```python
import jax
import jax.numpy as jnp
from jax import lax
from jax.experimental import pallas as pl
from jax.experimental.pallas import tpu as pltpu
from jax.sharding import PartitionSpec as P

LOSS_SCALE = 64.0
BETA_ONE = 0.9
BETA_TWO = 0.95
LEARN_RATE = 0.002
DECAY = 0.1
EPSILON = 1e-08
STEP_COUNT = 20.0

D = 2048
FF = 768
ROWS = 512
FWD_ROWS = 1024
EXPERTS = 32
DEVICES = 128
CAP = 8
SLOTS = DEVICES * CAP
OWN = FF // DEVICES
BLOCK = OWN * D // 8
HALVES = D // 1024
SEND_ONE = FF + D + BLOCK
SEND_TWO = FF + BLOCK
LANES = 256
MIB = 1 << 20

BF16 = jnp.bfloat16
F32 = jnp.float32
I32 = jnp.int32


def iota(shape, dim):
    return lax.broadcasted_iota(I32, shape, dim)


def mm(a, b, dims=((1,), (0,))):
    return lax.dot_general(a, b, (dims, ((), ())), preferred_element_type=F32)


def pick_rows(place_row):
    shape = (SLOTS, DEVICES)
    spread = jnp.where(iota(shape, 0) // 8 == iota(shape, 1), place_row, 0)
    mine = jnp.sum(spread.astype(F32), axis=1, keepdims=True).astype(I32)
    shape = (SLOTS, 8 * EXPERTS)
    row, col = iota(shape, 0), iota(shape, 1)
    hit = (col % EXPERTS == mine) & (col // EXPERTS == row % 8)
    return jnp.where(hit, 1.0, 0.0).astype(BF16)


def pick_columns(place_row):
    shape = (DEVICES, SLOTS)
    wide = jnp.where(iota(shape, 1) // 8 == iota(shape, 0), 1.0, 0.0).astype(BF16)
    mine = mm(place_row.astype(F32).astype(BF16), wide).astype(I32)
    shape = (8 * EXPERTS, SLOTS)
    row, col = iota(shape, 0), iota(shape, 1)
    hit = (row % EXPERTS == mine) & (row // EXPERTS == col % 8)
    return jnp.where(hit, 1.0, 0.0).astype(BF16)


def block_order(to_blocks):
    size = 8 * 8 * OWN
    shape = (size, size)
    blk, mat = (iota(shape, 0), iota(shape, 1)) if to_blocks else (iota(shape, 1), iota(shape, 0))
    target = (blk % 8) * (8 * OWN) + (blk // 8 % 8) * OWN + blk // 64
    return jnp.where(target == mat, 1.0, 0.0).astype(BF16)


def copies(pairs, sems, first=0):
    made = [pltpu.make_async_copy(a, b, sems.at[first + k]) for k, (a, b) in enumerate(pairs)]
    for copy in made:
        copy.start()
    return made


def lanes(k, width=LANES):
    return pl.ds(k * width, width)


NEAR, FAR = pltpu.VMEM, pltpu.HBM


def call(kernel, ins, outs, scratch, mib, flops, moved, name, **more):
    near = pl.BlockSpec(memory_space=NEAR)
    far = pl.BlockSpec(memory_space=pl.ANY)
    run = pl.pallas_call(
        kernel,
        in_specs=[near if space is NEAR else far for _, space in ins],
        out_specs=[near if space is NEAR else far for space, _, _ in outs],
        out_shape=[space(shape, kind) for space, shape, kind in outs],
        scratch_shapes=scratch,
        compiler_params=pltpu.CompilerParams(vmem_limit_bytes=mib * MIB),
        cost_estimate=pl.CostEstimate(flops=flops, bytes_accessed=moved, transcendentals=0),
        name=name,
        **more,
    )
    return run(*[pltpu.with_memory_space_constraint(x, space) for x, space in ins])


def matrix_half(blocks, start, weight, perm, h):
    for pair in range(DEVICES // 16):
        stacked = jnp.concatenate(
            [
                jnp.concatenate(
                    [
                        blocks[pl.ds((pair * 2 + g) * 64, 64), pl.ds(start + (h * OWN + f) * 128, 128)]
                        for g in range(2)
                    ],
                    axis=1,
                )
                for f in range(OWN)
            ],
            axis=0,
        )
        moved = mm(perm, stacked).astype(BF16)
        for g in range(2):
            for s in range(8):
                weight[pl.ds((pair * 2 + g) * 8 * OWN, 8 * OWN), pl.ds((h * 8 + s) * 128, 128)] = moved[
                    s * 8 * OWN : (s + 1) * 8 * OWN, g * 128 : (g + 1) * 128
                ]


def blocks_half(matrix, blocks, perm, h, done):
    for pair in range(DEVICES // 16):
        stacked = jnp.concatenate(
            [
                jnp.concatenate(
                    [
                        matrix[pl.ds((pair * 2 + g) * 8 * OWN, 8 * OWN), pl.ds((h * 8 + s) * 128, 128)]
                        for g in range(2)
                    ],
                    axis=1,
                )
                for s in range(8)
            ],
            axis=0,
        )
        moved = mm(perm, stacked).astype(BF16)
        for g in range(2):
            for f in range(OWN):
                blocks[pl.ds((pair * 2 + g) * 64, 64), pl.ds((h * OWN + f) * 128, 128)] = moved[
                    f * 64 : (f + 1) * 64, g * 128 : (g + 1) * 128
                ]
        done(pair)


def stacked_master(block):
    return jnp.concatenate(
        [
            jnp.concatenate(
                [block[:, (h * 8 + s) * 128 : (h * 8 + s + 1) * 128] for h in range(HALVES)], axis=1
            )
            for s in range(8)
        ],
        axis=0,
    )


def dispatch_kernel(
    route, place, saved, grad, master, send, position, route_v, place_v, saved_v, grad_v, master_v, position_v, sems
):
    got_route, got_place, got_saved, got_grad, got_master = copies(
        [(route, route_v), (place, place_v), (saved, saved_v), (grad, grad_v), (master, master_v)], sems
    )
    got_route.wait()
    target = route_v[...]
    ones = jnp.where(iota((DEVICES, ROWS), 0) == target, 1.0, 0.0)
    shape = (ROWS, ROWS)
    upto = jnp.where(iota(shape, 0) < iota(shape, 1), 1.0, 0.0).astype(BF16)
    earlier = mm(ones.astype(BF16), upto)
    rank = jnp.sum(ones * earlier, axis=0, keepdims=True).astype(I32)
    where = target * CAP + rank
    position_v[...] = where
    (told,) = copies([(position_v, position)], sems, 5)
    slot_of = jnp.where(iota((SLOTS, ROWS), 0) == where, 1.0, 0.0).astype(BF16)
    got_place.wait()
    pick = pick_rows(place_v[...])
    got_saved.wait()
    for k in range(3):
        send[:, lanes(k)] = mm(slot_of, saved_v[:, lanes(k)]).astype(BF16)
    got_grad.wait()
    for k in range(8):
        send[:, lanes(3 + k)] = mm(slot_of, grad_v[:, lanes(k)]).astype(BF16)
    got_master.wait()
    for f in range(OWN):
        rows = stacked_master(master_v[:, lanes(f, D)]).astype(BF16)
        picked = mm(pick, rows).astype(BF16)
        for h in range(HALVES):
            send[:, lanes(22 + h * OWN + f, 128)] = picked[:, h * 128 : (h + 1) * 128]
    told.wait()


def dispatch(route, place, saved, grad, master):
    return call(
        dispatch_kernel,
        [(route, FAR), (place, FAR), (saved, FAR), (grad, FAR), (master, FAR)],
        [(NEAR, (SLOTS, SEND_ONE), BF16), (FAR, (1, ROWS), I32)],
        [
            pltpu.VMEM((1, ROWS), I32),
            pltpu.VMEM((1, DEVICES), I32),
            pltpu.VMEM((ROWS, FF), BF16),
            pltpu.VMEM((ROWS, D), BF16),
            pltpu.VMEM((EXPERTS, OWN * D), F32),
            pltpu.VMEM((1, ROWS), I32),
            pltpu.SemaphoreType.DMA((6,)),
        ],
        16,
        4_000_000_000,
        14_000_000,
        "dispatch_rows",
    )


def partial_kernel(got, out, part_v, out_v, sems):
    perm = block_order(True)
    left = got[:, pl.ds(0, FF)].T
    sent = []
    for h in range(HALVES):
        for k in range(4 * h, 4 * h + 4):
            part_v[:, lanes(k)] = (mm(left, got[:, lanes(3 + k)]) * (1.0 / LOSS_SCALE)).astype(BF16)

        def ship(pair, h=h):
            if pair % 2:
                at = (lanes(pair // 2), lanes(h, BLOCK // HALVES))
                sent.extend(copies([(out_v.at[at], out.at[at])], sems, 4 * h + pair // 2))

        blocks_half(part_v, out_v, perm, h, ship)
    for copy in sent:
        copy.wait()


def partials(got):
    return call(
        partial_kernel,
        [(got, NEAR)],
        [(FAR, (SLOTS, BLOCK), BF16)],
        [
            pltpu.VMEM((FF, D), BF16),
            pltpu.VMEM((SLOTS, BLOCK), BF16),
            pltpu.SemaphoreType.DMA((4 * HALVES,)),
        ],
        20,
        4_400_000_000,
        9_000_000,
        "partial_blocks",
    )[0]


def input_kernel(
    position, rows, got, out, back, ordered, position_v, rows_v, weight, out_v, back_v, ordered_v, sems
):
    got_position, got_rows = copies([(position, position_v), (rows, rows_v)], sems)
    perm = block_order(False)
    for h in range(HALVES):
        matrix_half(got, FF + D, weight, perm, h)
    sent = []
    for k in range(4):
        tall = pl.ds(k * 256, 256)
        out_v[tall, :] = mm(got[tall, pl.ds(FF, D)], weight[...], ((1,), (1,))).astype(BF16)
        sent += copies([(out_v.at[tall, :], out.at[tall, :])], sems, 2 + k)
    got_position.wait()
    shape = (ROWS, ROWS)
    spread = jnp.where(iota(shape, 0) == iota(shape, 1), position_v[...], 0)
    where = jnp.sum(spread.astype(F32), axis=1, keepdims=True).astype(I32)
    back_v[...] = jnp.where(iota((ROWS, SLOTS), 1) == where, 1.0, 0.0).astype(BF16)
    sent += copies([(back_v, back)], sems, 6)
    got_rows.wait()
    shape = (FF, FF)
    natural, target = iota(shape, 0), iota(shape, 1)
    order = jnp.where(target % DEVICES * OWN + target // DEVICES == natural, 1.0, 0.0).astype(BF16)
    ordered_v[...] = mm(rows_v[...], order).astype(BF16)
    sent += copies([(ordered_v, ordered)], sems, 7)
    for copy in sent:
        copy.wait()


def input_parts(got, position, rows):
    return call(
        input_kernel,
        [(position, FAR), (rows, FAR), (got, NEAR)],
        [(FAR, (SLOTS, FF), BF16), (FAR, (ROWS, SLOTS), BF16), (FAR, rows.shape, BF16)],
        [
            pltpu.VMEM((1, ROWS), I32),
            pltpu.VMEM((FWD_ROWS, FF), BF16),
            pltpu.VMEM((FF, D), BF16),
            pltpu.VMEM((SLOTS, FF), BF16),
            pltpu.VMEM((ROWS, SLOTS), BF16),
            pltpu.VMEM((FWD_ROWS, FF), BF16),
            pltpu.SemaphoreType.DMA((8,)),
        ],
        20,
        4_400_000_000,
        12_000_000,
        "input_parts",
    )


def adam_kernel(
    place_now, place_next, arrived, returning, master, one, two, send, new_master, new_one, new_two,
    now_v, then_v, master_v, one_v, two_v, next_v, first_v, second_v, total_v, rows_v,
    place_sems, in_sems, out_sems,
):
    got_now, got_then = copies([(place_now, now_v), (place_next, then_v)], place_sems)
    landed = []
    for f in range(OWN):
        landed += copies(
            [(a.at[:, lanes(f, D)], b.at[:, lanes(f, D)]) for a, b in ((master, master_v), (one, one_v), (two, two_v))],
            in_sems,
            3 * f,
        )
    (merged,) = copies([(returning, send.at[:, pl.ds(0, FF)])], place_sems, 2)
    got_now.wait()
    total_v[...] = mm(pick_columns(now_v[...]), arrived[...])
    sent = []
    for f in range(OWN):
        for copy in landed[3 * f : 3 * f + 3]:
            copy.wait()
        for h in range(HALVES):
            mine = lanes(h * OWN + f, 128)
            for s in range(8):
                owned = pl.ds(s * EXPERTS, EXPERTS)
                at = pl.ds(f * D + (h * 8 + s) * 128, 128)
                gradient = total_v[owned, mine]
                weight = master_v[:, at]
                first = BETA_ONE * one_v[:, at] + (1.0 - BETA_ONE) * gradient
                second = BETA_TWO * two_v[:, at] + (1.0 - BETA_TWO) * gradient * gradient
                first_hat = first * (1.0 / (1.0 - BETA_ONE**STEP_COUNT))
                second_hat = second * (1.0 / (1.0 - BETA_TWO**STEP_COUNT))
                updated = weight - LEARN_RATE * (first_hat / (jnp.sqrt(second_hat) + EPSILON) + DECAY * weight)
                first_v[:, at] = first
                second_v[:, at] = second
                next_v[:, at] = updated
                rows_v[owned, mine] = updated.astype(BF16)
        sent += copies(
            [
                (a.at[:, lanes(f, D)], b.at[:, lanes(f, D)])
                for a, b in ((next_v, new_master), (first_v, new_one), (second_v, new_two))
            ],
            out_sems,
            3 * f,
        )
    got_then.wait()
    send[:, pl.ds(FF, BLOCK)] = mm(pick_rows(then_v[...]), rows_v[...]).astype(BF16)
    for copy in [merged] + sent:
        copy.wait()


def adam(place_now, place_next, arrived, returning, master, one, two):
    state = (FAR, master.shape, F32)
    flat = pltpu.VMEM((EXPERTS, OWN * D), F32)
    return call(
        adam_kernel,
        [(x, NEAR if x is arrived else FAR) for x in (place_now, place_next, arrived, returning, master, one, two)],
        [(NEAR, (SLOTS, SEND_TWO), BF16), state, state, state],
        [pltpu.VMEM((1, DEVICES), I32)] * 2
        + [flat] * 6
        + [pltpu.VMEM((8 * EXPERTS, BLOCK), F32), pltpu.VMEM((8 * EXPERTS, BLOCK), BF16)]
        + [pltpu.SemaphoreType.DMA((3,))]
        + [pltpu.SemaphoreType.DMA((3 * OWN,))] * 2,
        24,
        1_700_000_000,
        16_000_000,
        "adam_step",
    )


def ordered_half(blocks, start, weight, perm, h):
    for g in range(DEVICES // 16):
        moved = mm(perm, blocks[pl.ds(g * 128, 128), pl.ds(start + h * OWN * 128, OWN * 128)]).astype(BF16)
        for s in range(8):
            for f in range(OWN):
                weight[pl.ds(f * DEVICES + g * 16, 16), pl.ds((h * 8 + s) * 128, 128)] = moved[
                    s * 16 : (s + 1) * 16, f * 128 : (f + 1) * 128
                ]


def forward_kernel(landed, back, rows, out, input_grad, weight, out_v, grad_v, sems):
    shape = (128, 128)
    to, come = iota(shape, 0), iota(shape, 1)
    perm = jnp.where(to % 16 * 8 + to // 16 == come, 1.0, 0.0).astype(BF16)
    for h in range(HALVES):
        ordered_half(landed, FF, weight, perm, h)
    grad_v[...] = mm(back[...], landed[:, pl.ds(0, FF)]).astype(BF16)
    sent = copies([(grad_v, input_grad)], sems)
    for k in range(8):
        tall = lanes(k, FWD_ROWS // 8)
        out_v[tall, :] = mm(rows[tall, :], weight[...]).astype(BF16)
        sent += copies([(out_v.at[tall, :], out.at[tall, :])], sems, 1 + k)
    for copy in sent:
        copy.wait()


def forward(landed, back, rows):
    return call(
        forward_kernel,
        [(landed, NEAR), (back, NEAR), (rows, NEAR)],
        [(FAR, (FWD_ROWS, D), BF16), (FAR, (ROWS, FF), BF16)],
        [
            pltpu.VMEM((FF, D), BF16),
            pltpu.VMEM((FWD_ROWS, D), BF16),
            pltpu.VMEM((ROWS, FF), BF16),
            pltpu.SemaphoreType.DMA((9,)),
        ],
        24,
        5_200_000_000,
        13_000_000,
        "forward_rows",
    )


def exchange(blocks):
    split = blocks.reshape(DEVICES, 8, blocks.shape[1])
    moved = lax.all_to_all(split, ("expert", "opt"), split_axis=0, concat_axis=0, tiled=True)
    return moved.reshape(blocks.shape)


def per_device(out_grad, saved_input, route, place_now, place_next, master, moment_one, moment_two, fwd_input):
    now, then = place_now.reshape(1, DEVICES), place_next.reshape(1, DEVICES)
    send, position = dispatch(route.reshape(1, ROWS), now, saved_input, out_grad, master)
    got = exchange(send)
    arrived = exchange(partials(got))
    returning, back, rows = input_parts(got, position, fwd_input)
    sending, new_master, new_one, new_two = adam(
        now, then, arrived, returning, master, moment_one, moment_two
    )
    landed = exchange(sending)
    fwd_output, input_grad = forward(landed, back, rows)
    return (input_grad, new_master, new_one, new_two, fwd_output)


def solution(mesh):
    split_rows = P(("expert", "opt"), None)
    split_columns = P(None, ("expert", "opt"))
    return jax.shard_map(
        per_device,
        mesh=mesh,
        in_specs=(split_rows, split_rows, split_rows, P(), P())
        + (split_columns, split_columns, split_columns, split_rows),
        out_specs=(split_rows, split_columns, split_columns, split_columns, split_rows),
        check_vma=False,
    )
```

```python
import jax
import jax.numpy as jnp
from jax import lax
from jax.experimental import pallas as pl
from jax.experimental.pallas import tpu as pltpu
from jax.sharding import PartitionSpec as P

LOSS_SCALE = 64.0
BETA_ONE = 0.9
BETA_TWO = 0.95
LEARN_RATE = 0.002
DECAY = 0.1
EPSILON = 1e-08
STEP_COUNT = 20.0

D = 2048
FF = 768
ROWS = 512
FWD_ROWS = 1024
EXPERTS = 32
DEVICES = 128
CAP = 8
SLOTS = DEVICES * CAP
OWN = FF // DEVICES
BLOCK = OWN * D // 8
HALVES = D // 1024
SEND_ONE = FF + D + BLOCK
SEND_TWO = FF + BLOCK
LANES = 256
MIB = 1 << 20

BF16 = jnp.bfloat16
F32 = jnp.float32
I32 = jnp.int32


def iota(shape, dim):
    return lax.broadcasted_iota(I32, shape, dim)


def mm(a, b, dims=((1,), (0,))):
    return lax.dot_general(a, b, (dims, ((), ())), preferred_element_type=F32)


def pick_rows(place_row):
    shape = (SLOTS, DEVICES)
    spread = jnp.where(iota(shape, 0) // 8 == iota(shape, 1), place_row, 0)
    mine = jnp.sum(spread.astype(F32), axis=1, keepdims=True).astype(I32)
    shape = (SLOTS, 8 * EXPERTS)
    row, col = iota(shape, 0), iota(shape, 1)
    hit = (col % EXPERTS == mine) & (col // EXPERTS == row % 8)
    return jnp.where(hit, 1.0, 0.0).astype(BF16)


def pick_columns(place_row):
    shape = (DEVICES, SLOTS)
    wide = jnp.where(iota(shape, 1) // 8 == iota(shape, 0), 1.0, 0.0).astype(BF16)
    mine = mm(place_row.astype(F32).astype(BF16), wide).astype(I32)
    shape = (8 * EXPERTS, SLOTS)
    row, col = iota(shape, 0), iota(shape, 1)
    hit = (row % EXPERTS == mine) & (row // EXPERTS == col % 8)
    return jnp.where(hit, 1.0, 0.0).astype(BF16)


def block_order(to_blocks):
    size = 8 * 8 * OWN
    shape = (size, size)
    blk, mat = (iota(shape, 0), iota(shape, 1)) if to_blocks else (iota(shape, 1), iota(shape, 0))
    target = (blk % 8) * (8 * OWN) + (blk // 8 % 8) * OWN + blk // 64
    return jnp.where(target == mat, 1.0, 0.0).astype(BF16)


def copies(pairs, sems, first=0):
    made = [pltpu.make_async_copy(a, b, sems.at[first + k]) for k, (a, b) in enumerate(pairs)]
    for copy in made:
        copy.start()
    return made


def lanes(k, width=LANES):
    return pl.ds(k * width, width)


NEAR, FAR = pltpu.VMEM, pltpu.HBM


def call(kernel, ins, outs, scratch, mib, flops, moved, name, **more):
    near = pl.BlockSpec(memory_space=NEAR)
    far = pl.BlockSpec(memory_space=pl.ANY)
    run = pl.pallas_call(
        kernel,
        in_specs=[near if space is NEAR else far for _, space in ins],
        out_specs=[near if space is NEAR else far for space, _, _ in outs],
        out_shape=[space(shape, kind) for space, shape, kind in outs],
        scratch_shapes=scratch,
        compiler_params=pltpu.CompilerParams(vmem_limit_bytes=mib * MIB),
        cost_estimate=pl.CostEstimate(flops=flops, bytes_accessed=moved, transcendentals=0),
        name=name,
        **more,
    )
    return run(*[pltpu.with_memory_space_constraint(x, space) for x, space in ins])


def matrix_half(blocks, start, weight, perm, h):
    for pair in range(DEVICES // 16):
        stacked = jnp.concatenate(
            [
                jnp.concatenate(
                    [
                        blocks[pl.ds((pair * 2 + g) * 64, 64), pl.ds(start + (h * OWN + f) * 128, 128)]
                        for g in range(2)
                    ],
                    axis=1,
                )
                for f in range(OWN)
            ],
            axis=0,
        )
        moved = mm(perm, stacked).astype(BF16)
        for g in range(2):
            for s in range(8):
                weight[pl.ds((pair * 2 + g) * 8 * OWN, 8 * OWN), pl.ds((h * 8 + s) * 128, 128)] = moved[
                    s * 8 * OWN : (s + 1) * 8 * OWN, g * 128 : (g + 1) * 128
                ]


def blocks_half(matrix, blocks, perm, h, done):
    for pair in range(DEVICES // 16):
        stacked = jnp.concatenate(
            [
                jnp.concatenate(
                    [
                        matrix[pl.ds((pair * 2 + g) * 8 * OWN, 8 * OWN), pl.ds((h * 8 + s) * 128, 128)]
                        for g in range(2)
                    ],
                    axis=1,
                )
                for s in range(8)
            ],
            axis=0,
        )
        moved = mm(perm, stacked).astype(BF16)
        for g in range(2):
            for f in range(OWN):
                blocks[pl.ds((pair * 2 + g) * 64, 64), pl.ds((h * OWN + f) * 128, 128)] = moved[
                    f * 64 : (f + 1) * 64, g * 128 : (g + 1) * 128
                ]
        done(pair)


def interleave(inner, outer, back):
    shape = (inner * outer, inner * outer)
    a, b = (iota(shape, 1), iota(shape, 0)) if back else (iota(shape, 0), iota(shape, 1))
    return jnp.where(a % outer * inner + a // outer == b, 1.0, 0.0).astype(BF16)


def stacked_master(block):
    return jnp.concatenate(
        [
            jnp.concatenate(
                [block[:, (h * 8 + s) * 128 : (h * 8 + s + 1) * 128] for h in range(HALVES)], axis=1
            )
            for s in range(8)
        ],
        axis=0,
    )


def dispatch_kernel(
    route, place, saved, grad, master, send, position, route_v, place_v, saved_v, grad_v, master_v, position_v, sems
):
    got_route, got_place, got_saved, got_grad, got_master = copies(
        [(route, route_v), (place, place_v), (saved, saved_v), (grad, grad_v), (master, master_v)], sems
    )
    got_route.wait()
    target = route_v[...]
    ones = jnp.where(iota((DEVICES, ROWS), 0) == target, 1.0, 0.0)
    shape = (ROWS, ROWS)
    upto = jnp.where(iota(shape, 0) < iota(shape, 1), 1.0, 0.0).astype(BF16)
    earlier = mm(ones.astype(BF16), upto)
    rank = jnp.sum(ones * earlier, axis=0, keepdims=True).astype(I32)
    where = target * CAP + rank
    position_v[...] = where
    (told,) = copies([(position_v, position)], sems, 5)
    slot_of = jnp.where(iota((SLOTS, ROWS), 0) == where, 1.0, 0.0).astype(BF16)
    got_saved.wait()
    send[:, pl.ds(0, FF)] = mm(slot_of, saved_v[...]).astype(BF16)
    got_grad.wait()
    for k in range(2):
        tall = slice(k * SLOTS // 2, (k + 1) * SLOTS // 2)
        send[tall, pl.ds(FF, D)] = mm(slot_of[tall], grad_v[...]).astype(BF16)
    got_place.wait()
    got_master.wait()
    pick = pick_rows(place_v[...])
    for f in range(OWN):
        rows = stacked_master(master_v[:, lanes(f, D)]).astype(BF16)
        picked = mm(pick, rows).astype(BF16)
        for h in range(HALVES):
            send[:, lanes(22 + h * OWN + f, 128)] = picked[:, h * 128 : (h + 1) * 128]
    told.wait()


def dispatch(route, place, saved, grad, master):
    return call(
        dispatch_kernel,
        [(route, FAR), (place, FAR), (saved, FAR), (grad, FAR), (master, FAR)],
        [(NEAR, (SLOTS, SEND_ONE), BF16), (FAR, (1, ROWS), I32)],
        [
            pltpu.VMEM((1, ROWS), I32),
            pltpu.VMEM((1, DEVICES), I32),
            pltpu.VMEM((ROWS, FF), BF16),
            pltpu.VMEM((ROWS, D), BF16),
            pltpu.VMEM((EXPERTS, OWN * D), F32),
            pltpu.VMEM((1, ROWS), I32),
            pltpu.SemaphoreType.DMA((6,)),
        ],
        16,
        4_000_000_000,
        14_000_000,
        "dispatch_rows",
    )


def partial_kernel(got, out, part_v, out_v, sems):
    perm = block_order(True)
    left = got[:, pl.ds(0, FF)].T
    sent = []
    for h in range(HALVES):
        for k in range(4 * h, 4 * h + 4):
            part_v[:, lanes(k)] = (mm(left, got[:, lanes(3 + k)]) * (1.0 / LOSS_SCALE)).astype(BF16)

        def ship(pair, h=h):
            if pair % 2:
                at = (lanes(pair // 2), lanes(h, BLOCK // HALVES))
                sent.extend(copies([(out_v.at[at], out.at[at])], sems, 4 * h + pair // 2))

        blocks_half(part_v, out_v, perm, h, ship)
    for copy in sent:
        copy.wait()


def partials(got):
    return call(
        partial_kernel,
        [(got, NEAR)],
        [(FAR, (SLOTS, BLOCK), BF16)],
        [
            pltpu.VMEM((FF, D), BF16),
            pltpu.VMEM((SLOTS, BLOCK), BF16),
            pltpu.SemaphoreType.DMA((4 * HALVES,)),
        ],
        20,
        4_400_000_000,
        9_000_000,
        "partial_blocks",
    )[0]


def input_kernel(
    position, rows, got, out, back, ordered, position_v, rows_v, weight, out_v, back_v, ordered_v, sems
):
    got_position, got_rows = copies([(position, position_v), (rows, rows_v)], sems)
    perm = block_order(False)
    for h in range(HALVES):
        matrix_half(got, FF + D, weight, perm, h)
    sent = []
    for k in range(4):
        tall = pl.ds(k * 256, 256)
        out_v[tall, :] = mm(got[tall, pl.ds(FF, D)], weight[...], ((1,), (1,))).astype(BF16)
        sent += copies([(out_v.at[tall, :], out.at[tall, :])], sems, 2 + k)
    got_position.wait()
    shape = (ROWS, ROWS)
    spread = jnp.where(iota(shape, 0) == iota(shape, 1), position_v[...], 0)
    where = jnp.sum(spread.astype(F32), axis=1, keepdims=True).astype(I32)
    back_v[...] = jnp.where(iota((ROWS, SLOTS), 1) == where, 1.0, 0.0).astype(BF16)
    sent += copies([(back_v, back)], sems, 6)
    got_rows.wait()
    shape = (FF, FF)
    natural, target = iota(shape, 0), iota(shape, 1)
    order = jnp.where(target % DEVICES * OWN + target // DEVICES == natural, 1.0, 0.0).astype(BF16)
    ordered_v[...] = mm(rows_v[...], order).astype(BF16)
    sent += copies([(ordered_v, ordered)], sems, 7)
    for copy in sent:
        copy.wait()


def input_parts(got, position, rows):
    return call(
        input_kernel,
        [(position, FAR), (rows, FAR), (got, NEAR)],
        [(FAR, (SLOTS, FF), BF16), (FAR, (ROWS, SLOTS), BF16), (FAR, rows.shape, BF16)],
        [
            pltpu.VMEM((1, ROWS), I32),
            pltpu.VMEM((FWD_ROWS, FF), BF16),
            pltpu.VMEM((FF, D), BF16),
            pltpu.VMEM((SLOTS, FF), BF16),
            pltpu.VMEM((ROWS, SLOTS), BF16),
            pltpu.VMEM((FWD_ROWS, FF), BF16),
            pltpu.SemaphoreType.DMA((8,)),
        ],
        20,
        4_400_000_000,
        12_000_000,
        "input_parts",
    )


def adam_kernel(
    place_now, place_next, arrived, returning, master, one, two, send, new_master, new_one, new_two,
    now_v, then_v, master_v, one_v, two_v, total_v, rows_v, place_sems, in_sems,
):
    got_now, got_then = copies([(place_now, now_v), (place_next, then_v)], place_sems)
    landed = []
    for f in range(OWN):
        landed += copies(
            [(a.at[:, lanes(f, D)], b.at[:, lanes(f, D)]) for a, b in ((master, master_v), (one, one_v), (two, two_v))],
            in_sems,
            3 * f,
        )
    (merged,) = copies([(returning, send.at[:, pl.ds(0, FF)])], place_sems, 2)
    got_now.wait()
    total_v[...] = mm(pick_columns(now_v[...]), arrived[...])
    for f in range(OWN):
        for copy in landed[3 * f : 3 * f + 3]:
            copy.wait()
        for h in range(HALVES):
            mine = lanes(h * OWN + f, 128)
            for s in range(8):
                owned = pl.ds(s * EXPERTS, EXPERTS)
                at = pl.ds(f * D + (h * 8 + s) * 128, 128)
                gradient = total_v[owned, mine]
                weight = master_v[:, at]
                first = BETA_ONE * one_v[:, at] + (1.0 - BETA_ONE) * gradient
                second = BETA_TWO * two_v[:, at] + (1.0 - BETA_TWO) * gradient * gradient
                second_hat = second * (1.0 / (1.0 - BETA_TWO**STEP_COUNT))
                root = second_hat * lax.rsqrt(second_hat)
                step = first * (LEARN_RATE / (1.0 - BETA_ONE**STEP_COUNT)) / (root + EPSILON)
                updated = weight * (1.0 - LEARN_RATE * DECAY) - step
                new_one[:, at] = first
                new_two[:, at] = second
                new_master[:, at] = updated
                rows_v[owned, mine] = updated.astype(BF16)
    got_then.wait()
    send[:, pl.ds(FF, BLOCK)] = mm(pick_rows(then_v[...]), rows_v[...]).astype(BF16)
    merged.wait()


def adam(place_now, place_next, arrived, returning, master, one, two):
    state = (NEAR, master.shape, F32)
    flat = pltpu.VMEM((EXPERTS, OWN * D), F32)
    return call(
        adam_kernel,
        [(x, NEAR if x is arrived else FAR) for x in (place_now, place_next, arrived, returning, master, one, two)],
        [(NEAR, (SLOTS, SEND_TWO), BF16), state, state, state],
        [pltpu.VMEM((1, DEVICES), I32)] * 2
        + [flat] * 3
        + [pltpu.VMEM((8 * EXPERTS, BLOCK), F32), pltpu.VMEM((8 * EXPERTS, BLOCK), BF16)]
        + [pltpu.SemaphoreType.DMA((3,))]
        + [pltpu.SemaphoreType.DMA((3 * OWN,))],
        16,
        1_700_000_000,
        16_000_000,
        "adam_step",
    )


def ordered_half(blocks, start, weight, perm, h):
    for g in range(DEVICES // 16):
        moved = mm(perm, blocks[pl.ds(g * 128, 128), pl.ds(start + h * OWN * 128, OWN * 128)]).astype(BF16)
        for s in range(8):
            for f in range(OWN):
                weight[pl.ds(f * DEVICES + g * 16, 16), pl.ds((h * 8 + s) * 128, 128)] = moved[
                    s * 16 : (s + 1) * 16, f * 128 : (f + 1) * 128
                ]


def forward_kernel(
    landed, back, rows, master, one, two, out, input_grad, new_master, new_one, new_two, weight, out_v, grad_v, sems
):
    kept = copies([(master, new_master), (one, new_one), (two, new_two)], sems, 9)
    perm = interleave(8, 16, False)
    for h in range(HALVES):
        ordered_half(landed, FF, weight, perm, h)
    grad_v[...] = mm(back[...], landed[:, pl.ds(0, FF)]).astype(BF16)
    sent = copies([(grad_v, input_grad)], sems)
    for k in range(8):
        tall = lanes(k, FWD_ROWS // 8)
        out_v[tall, :] = mm(rows[tall, :], weight[...]).astype(BF16)
        sent += copies([(out_v.at[tall, :], out.at[tall, :])], sems, 1 + k)
    for copy in kept + sent:
        copy.wait()


def forward(landed, back, rows, *states):
    return call(
        forward_kernel,
        [(x, NEAR) for x in (landed, back, rows) + states],
        [(FAR, (FWD_ROWS, D), BF16), (FAR, (ROWS, FF), BF16)] + [(FAR, x.shape, F32) for x in states],
        [
            pltpu.VMEM((FF, D), BF16),
            pltpu.VMEM((FWD_ROWS, D), BF16),
            pltpu.VMEM((ROWS, FF), BF16),
            pltpu.SemaphoreType.DMA((12,)),
        ],
        24,
        5_200_000_000,
        13_000_000,
        "forward_rows",
    )


def exchange(blocks):
    split = blocks.reshape(DEVICES, 8, blocks.shape[1])
    moved = lax.all_to_all(split, ("expert", "opt"), split_axis=0, concat_axis=0, tiled=True)
    return moved.reshape(blocks.shape)


def per_device(out_grad, saved_input, route, place_now, place_next, master, moment_one, moment_two, fwd_input):
    now, then = place_now.reshape(1, DEVICES), place_next.reshape(1, DEVICES)
    send, position = dispatch(route.reshape(1, ROWS), now, saved_input, out_grad, master)
    got = exchange(send)
    arrived = exchange(partials(got))
    returning, back, rows = input_parts(got, position, fwd_input)
    sending, *states = adam(now, then, arrived, returning, master, moment_one, moment_two)
    landed = exchange(sending)
    fwd_output, input_grad, new_master, new_one, new_two = forward(landed, back, rows, *states)
    return (input_grad, new_master, new_one, new_two, fwd_output)


def solution(mesh):
    split_rows = P(("expert", "opt"), None)
    split_columns = P(None, ("expert", "opt"))
    return jax.shard_map(
        per_device,
        mesh=mesh,
        in_specs=(split_rows, split_rows, split_rows, P(), P())
        + (split_columns, split_columns, split_columns, split_rows),
        out_specs=(split_rows, split_columns, split_columns, split_columns, split_rows),
        check_vma=False,
    )
```

```python
import jax
import jax.numpy as jnp
from jax import lax
from jax.experimental import pallas as pl
from jax.experimental.pallas import tpu as pltpu
from jax.sharding import PartitionSpec as P

LOSS_SCALE = 64.0
BETA_ONE = 0.9
BETA_TWO = 0.95
LEARN_RATE = 0.002
DECAY = 0.1
EPSILON = 1e-08
STEP_COUNT = 20.0

D = 2048
FF = 768
ROWS = 512
FWD_ROWS = 1024
EXPERTS = 32
DEVICES = 128
CAP = 8
SLOTS = DEVICES * CAP
OWN = FF // DEVICES
BLOCK = OWN * D // 8
HALVES = D // 1024
SEND_ONE = FF + D + BLOCK
SEND_TWO = FF + BLOCK
LANES = 256
MIB = 1 << 20

BF16 = jnp.bfloat16
F32 = jnp.float32
I32 = jnp.int32


def iota(shape, dim):
    return lax.broadcasted_iota(I32, shape, dim)


def mm(a, b, dims=((1,), (0,))):
    return lax.dot_general(a, b, (dims, ((), ())), preferred_element_type=F32)


def pick_rows(place_row):
    shape = (SLOTS, DEVICES)
    spread = jnp.where(iota(shape, 0) // 8 == iota(shape, 1), place_row, 0)
    mine = jnp.sum(spread.astype(F32), axis=1, keepdims=True).astype(I32)
    shape = (SLOTS, 8 * EXPERTS)
    row, col = iota(shape, 0), iota(shape, 1)
    hit = (col % EXPERTS == mine) & (col // EXPERTS == row % 8)
    return jnp.where(hit, 1.0, 0.0).astype(BF16)


def pick_columns(place_row):
    shape = (DEVICES, SLOTS)
    wide = jnp.where(iota(shape, 1) // 8 == iota(shape, 0), 1.0, 0.0).astype(BF16)
    mine = mm(place_row.astype(F32).astype(BF16), wide).astype(I32)
    shape = (8 * EXPERTS, SLOTS)
    row, col = iota(shape, 0), iota(shape, 1)
    hit = (row % EXPERTS == mine) & (row // EXPERTS == col % 8)
    return jnp.where(hit, 1.0, 0.0).astype(BF16)


def block_order(to_blocks):
    size = 8 * 8 * OWN
    shape = (size, size)
    blk, mat = (iota(shape, 0), iota(shape, 1)) if to_blocks else (iota(shape, 1), iota(shape, 0))
    target = (blk % 8) * (8 * OWN) + (blk // 8 % 8) * OWN + blk // 64
    return jnp.where(target == mat, 1.0, 0.0).astype(BF16)


def copies(pairs, sems, first=0):
    made = [pltpu.make_async_copy(a, b, sems.at[first + k]) for k, (a, b) in enumerate(pairs)]
    for copy in made:
        copy.start()
    return made


def lanes(k, width=LANES):
    return pl.ds(k * width, width)


NEAR, FAR = pltpu.VMEM, pltpu.HBM


def call(kernel, ins, outs, scratch, mib, flops, moved, name, **more):
    near = pl.BlockSpec(memory_space=NEAR)
    far = pl.BlockSpec(memory_space=pl.ANY)
    run = pl.pallas_call(
        kernel,
        in_specs=[near if space is NEAR else far for _, space in ins],
        out_specs=[near if space is NEAR else far for space, _, _ in outs],
        out_shape=[space(shape, kind) for space, shape, kind in outs],
        scratch_shapes=scratch,
        compiler_params=pltpu.CompilerParams(vmem_limit_bytes=mib * MIB),
        cost_estimate=pl.CostEstimate(flops=flops, bytes_accessed=moved, transcendentals=0),
        name=name,
        **more,
    )
    return run(*[pltpu.with_memory_space_constraint(x, space) for x, space in ins])


def matrix_half(blocks, start, weight, perm, h):
    for pair in range(DEVICES // 16):
        stacked = jnp.concatenate(
            [
                jnp.concatenate(
                    [
                        blocks[pl.ds((pair * 2 + g) * 64, 64), pl.ds(start + (h * OWN + f) * 128, 128)]
                        for g in range(2)
                    ],
                    axis=1,
                )
                for f in range(OWN)
            ],
            axis=0,
        )
        moved = mm(perm, stacked).astype(BF16)
        for g in range(2):
            for s in range(8):
                weight[pl.ds((pair * 2 + g) * 8 * OWN, 8 * OWN), pl.ds((h * 8 + s) * 128, 128)] = moved[
                    s * 8 * OWN : (s + 1) * 8 * OWN, g * 128 : (g + 1) * 128
                ]


def blocks_half(matrix, blocks, perm, h, done):
    for pair in range(DEVICES // 16):
        stacked = jnp.concatenate(
            [
                jnp.concatenate(
                    [
                        matrix[pl.ds((pair * 2 + g) * 8 * OWN, 8 * OWN), pl.ds((h * 8 + s) * 128, 128)]
                        for g in range(2)
                    ],
                    axis=1,
                )
                for s in range(8)
            ],
            axis=0,
        )
        moved = mm(perm, stacked).astype(BF16)
        for g in range(2):
            for f in range(OWN):
                blocks[pl.ds((pair * 2 + g) * 64, 64), pl.ds((h * OWN + f) * 128, 128)] = moved[
                    f * 64 : (f + 1) * 64, g * 128 : (g + 1) * 128
                ]
        done(pair)


def interleave(inner, outer, back):
    shape = (inner * outer, inner * outer)
    a, b = (iota(shape, 1), iota(shape, 0)) if back else (iota(shape, 0), iota(shape, 1))
    return jnp.where(a % outer * inner + a // outer == b, 1.0, 0.0).astype(BF16)


def stacked_master(block):
    return jnp.concatenate(
        [
            jnp.concatenate(
                [block[:, (h * 8 + s) * 128 : (h * 8 + s + 1) * 128] for h in range(HALVES)], axis=1
            )
            for s in range(8)
        ],
        axis=0,
    )


def dispatch_kernel(
    route, place, saved, grad, master, send, position, route_v, place_v, saved_v, grad_v, master_v, position_v, sems
):
    got_route, got_place, got_saved, got_grad, got_master = copies(
        [(route, route_v), (place, place_v), (saved, saved_v), (grad, grad_v), (master, master_v)], sems
    )
    got_route.wait()
    target = route_v[...]
    ones = jnp.where(iota((DEVICES, ROWS), 0) == target, 1.0, 0.0)
    shape = (ROWS, ROWS)
    upto = jnp.where(iota(shape, 0) < iota(shape, 1), 1.0, 0.0).astype(BF16)
    earlier = mm(ones.astype(BF16), upto)
    rank = jnp.sum(ones * earlier, axis=0, keepdims=True).astype(I32)
    where = target * CAP + rank
    position_v[...] = where
    (told,) = copies([(position_v, position)], sems, 5)
    slot_of = jnp.where(iota((SLOTS, ROWS), 0) == where, 1.0, 0.0).astype(BF16)
    got_saved.wait()
    send[:, pl.ds(0, FF)] = mm(slot_of, saved_v[...]).astype(BF16)
    got_grad.wait()
    for k in range(2):
        tall = slice(k * SLOTS // 2, (k + 1) * SLOTS // 2)
        send[tall, pl.ds(FF, D)] = mm(slot_of[tall], grad_v[...]).astype(BF16)
    got_place.wait()
    got_master.wait()
    pick = pick_rows(place_v[...])
    for f in range(OWN):
        rows = stacked_master(master_v[:, lanes(f, D)]).astype(BF16)
        picked = mm(pick, rows).astype(BF16)
        for h in range(HALVES):
            send[:, lanes(22 + h * OWN + f, 128)] = picked[:, h * 128 : (h + 1) * 128]
    told.wait()


def dispatch(route, place, saved, grad, master):
    return call(
        dispatch_kernel,
        [(route, FAR), (place, FAR), (saved, FAR), (grad, FAR), (master, FAR)],
        [(NEAR, (SLOTS, SEND_ONE), BF16), (FAR, (1, ROWS), I32)],
        [
            pltpu.VMEM((1, ROWS), I32),
            pltpu.VMEM((1, DEVICES), I32),
            pltpu.VMEM((ROWS, FF), BF16),
            pltpu.VMEM((ROWS, D), BF16),
            pltpu.VMEM((EXPERTS, OWN * D), F32),
            pltpu.VMEM((1, ROWS), I32),
            pltpu.SemaphoreType.DMA((6,)),
        ],
        16,
        4_000_000_000,
        14_000_000,
        "dispatch_rows",
    )


def partial_kernel(got, out, part_v, out_v, sems):
    perm = block_order(True)
    left = got[:, pl.ds(0, FF)].T
    sent = []
    for h in range(HALVES):
        for m in range(2):
            tall = slice(m * FF // 2, (m + 1) * FF // 2)
            wide = mm(left[tall], got[:, pl.ds(FF + h * 1024, 1024)])
            part_v[tall, lanes(h, 1024)] = (wide * (1.0 / LOSS_SCALE)).astype(BF16)

        def ship(pair, h=h):
            if pair % 2:
                at = (lanes(pair // 2), lanes(h, BLOCK // HALVES))
                sent.extend(copies([(out_v.at[at], out.at[at])], sems, 4 * h + pair // 2))

        blocks_half(part_v, out_v, perm, h, ship)
    for copy in sent:
        copy.wait()


def partials(got):
    return call(
        partial_kernel,
        [(got, NEAR)],
        [(FAR, (SLOTS, BLOCK), BF16)],
        [
            pltpu.VMEM((FF, D), BF16),
            pltpu.VMEM((SLOTS, BLOCK), BF16),
            pltpu.SemaphoreType.DMA((4 * HALVES,)),
        ],
        20,
        4_400_000_000,
        9_000_000,
        "partial_blocks",
    )[0]


def input_kernel(
    position, rows, got, out, back, ordered, position_v, rows_v, weight, out_v, back_v, ordered_v, sems
):
    got_position, got_rows = copies([(position, position_v), (rows, rows_v)], sems)
    perm = block_order(False)
    for h in range(HALVES):
        matrix_half(got, FF + D, weight, perm, h)
    sent = []
    for k in range(4):
        tall = pl.ds(k * 256, 256)
        out_v[tall, :] = mm(got[tall, pl.ds(FF, D)], weight[...], ((1,), (1,))).astype(BF16)
        sent += copies([(out_v.at[tall, :], out.at[tall, :])], sems, 2 + k)
    got_position.wait()
    shape = (ROWS, ROWS)
    spread = jnp.where(iota(shape, 0) == iota(shape, 1), position_v[...], 0)
    where = jnp.sum(spread.astype(F32), axis=1, keepdims=True).astype(I32)
    back_v[...] = jnp.where(iota((ROWS, SLOTS), 1) == where, 1.0, 0.0).astype(BF16)
    sent += copies([(back_v, back)], sems, 6)
    got_rows.wait()
    shape = (FF, FF)
    natural, target = iota(shape, 0), iota(shape, 1)
    order = jnp.where(target % DEVICES * OWN + target // DEVICES == natural, 1.0, 0.0).astype(BF16)
    ordered_v[...] = mm(rows_v[...], order).astype(BF16)
    sent += copies([(ordered_v, ordered)], sems, 7)
    for copy in sent:
        copy.wait()


def input_parts(got, position, rows):
    return call(
        input_kernel,
        [(position, FAR), (rows, FAR), (got, NEAR)],
        [(FAR, (SLOTS, FF), BF16), (FAR, (ROWS, SLOTS), BF16), (FAR, rows.shape, BF16)],
        [
            pltpu.VMEM((1, ROWS), I32),
            pltpu.VMEM((FWD_ROWS, FF), BF16),
            pltpu.VMEM((FF, D), BF16),
            pltpu.VMEM((SLOTS, FF), BF16),
            pltpu.VMEM((ROWS, SLOTS), BF16),
            pltpu.VMEM((FWD_ROWS, FF), BF16),
            pltpu.SemaphoreType.DMA((8,)),
        ],
        20,
        4_400_000_000,
        12_000_000,
        "input_parts",
    )


def adam_kernel(
    place_now, place_next, arrived, returning, master, one, two, send, new_master, new_one, new_two,
    now_v, then_v, master_v, one_v, two_v, total_v, rows_v, place_sems, in_sems,
):
    got_now, got_then = copies([(place_now, now_v), (place_next, then_v)], place_sems)
    landed = []
    for f in range(OWN):
        landed += copies(
            [(a.at[:, lanes(f, D)], b.at[:, lanes(f, D)]) for a, b in ((master, master_v), (one, one_v), (two, two_v))],
            in_sems,
            3 * f,
        )
    (merged,) = copies([(returning, send.at[:, pl.ds(0, FF)])], place_sems, 2)
    got_now.wait()
    total_v[...] = mm(pick_columns(now_v[...]), arrived[...])
    for f in range(OWN):
        if f % 3 == 0:
            for copy in landed[3 * f : 3 * (f + 3)]:
                copy.wait()
        for h in range(HALVES):
            mine = lanes(h * OWN + f, 128)
            for s in range(8):
                owned = pl.ds(s * EXPERTS, EXPERTS)
                at = pl.ds(f * D + (h * 8 + s) * 128, 128)
                gradient = total_v[owned, mine]
                weight = master_v[:, at]
                first = BETA_ONE * one_v[:, at] + (1.0 - BETA_ONE) * gradient
                second = BETA_TWO * two_v[:, at] + (1.0 - BETA_TWO) * gradient * gradient
                second_hat = second * (1.0 / (1.0 - BETA_TWO**STEP_COUNT))
                root = second_hat * lax.rsqrt(second_hat)
                step = first * (LEARN_RATE / (1.0 - BETA_ONE**STEP_COUNT)) / (root + EPSILON)
                updated = weight * (1.0 - LEARN_RATE * DECAY) - step
                new_one[:, at] = first
                new_two[:, at] = second
                new_master[:, at] = updated
                rows_v[owned, mine] = updated.astype(BF16)
    got_then.wait()
    send[:, pl.ds(FF, BLOCK)] = mm(pick_rows(then_v[...]), rows_v[...]).astype(BF16)
    merged.wait()


def adam(place_now, place_next, arrived, returning, master, one, two):
    state = (NEAR, master.shape, F32)
    flat = pltpu.VMEM((EXPERTS, OWN * D), F32)
    return call(
        adam_kernel,
        [(x, NEAR if x is arrived else FAR) for x in (place_now, place_next, arrived, returning, master, one, two)],
        [(NEAR, (SLOTS, SEND_TWO), BF16), state, state, state],
        [pltpu.VMEM((1, DEVICES), I32)] * 2
        + [flat] * 3
        + [pltpu.VMEM((8 * EXPERTS, BLOCK), F32), pltpu.VMEM((8 * EXPERTS, BLOCK), BF16)]
        + [pltpu.SemaphoreType.DMA((3,))]
        + [pltpu.SemaphoreType.DMA((3 * OWN,))],
        16,
        1_700_000_000,
        16_000_000,
        "adam_step",
    )


def ordered_half(blocks, start, weight, perm, h):
    for g in range(DEVICES // 16):
        moved = mm(perm, blocks[pl.ds(g * 128, 128), pl.ds(start + h * OWN * 128, OWN * 128)]).astype(BF16)
        for s in range(8):
            for f in range(OWN):
                weight[pl.ds(f * DEVICES + g * 16, 16), pl.ds((h * 8 + s) * 128, 128)] = moved[
                    s * 16 : (s + 1) * 16, f * 128 : (f + 1) * 128
                ]


def forward_kernel(
    landed, back, rows, master, one, two, out, input_grad, new_master, new_one, new_two, weight, out_v, grad_v, sems
):
    kept = copies([(master, new_master), (one, new_one), (two, new_two)], sems, 9)
    perm = interleave(8, 16, False)
    for h in range(HALVES):
        ordered_half(landed, FF, weight, perm, h)
    grad_v[...] = mm(back[...], landed[:, pl.ds(0, FF)]).astype(BF16)
    sent = copies([(grad_v, input_grad)], sems)
    for k in range(8):
        tall = lanes(k, FWD_ROWS // 8)
        out_v[tall, :] = mm(rows[tall, :], weight[...]).astype(BF16)
        sent += copies([(out_v.at[tall, :], out.at[tall, :])], sems, 1 + k)
    for copy in kept + sent:
        copy.wait()


def forward(landed, back, rows, *states):
    return call(
        forward_kernel,
        [(x, NEAR) for x in (landed, back, rows) + states],
        [(FAR, (FWD_ROWS, D), BF16), (FAR, (ROWS, FF), BF16)] + [(FAR, x.shape, F32) for x in states],
        [
            pltpu.VMEM((FF, D), BF16),
            pltpu.VMEM((FWD_ROWS, D), BF16),
            pltpu.VMEM((ROWS, FF), BF16),
            pltpu.SemaphoreType.DMA((12,)),
        ],
        24,
        5_200_000_000,
        13_000_000,
        "forward_rows",
    )


def exchange(blocks):
    split = blocks.reshape(DEVICES, 8, blocks.shape[1])
    moved = lax.all_to_all(split, ("expert", "opt"), split_axis=0, concat_axis=0, tiled=True)
    return moved.reshape(blocks.shape)


def per_device(out_grad, saved_input, route, place_now, place_next, master, moment_one, moment_two, fwd_input):
    now, then = place_now.reshape(1, DEVICES), place_next.reshape(1, DEVICES)
    send, position = dispatch(route.reshape(1, ROWS), now, saved_input, out_grad, master)
    got = exchange(send)
    arrived = exchange(partials(got))
    returning, back, rows = input_parts(got, position, fwd_input)
    sending, *states = adam(now, then, arrived, returning, master, moment_one, moment_two)
    landed = exchange(sending)
    fwd_output, input_grad, new_master, new_one, new_two = forward(landed, back, rows, *states)
    return (input_grad, new_master, new_one, new_two, fwd_output)


def solution(mesh):
    split_rows = P(("expert", "opt"), None)
    split_columns = P(None, ("expert", "opt"))
    return jax.shard_map(
        per_device,
        mesh=mesh,
        in_specs=(split_rows, split_rows, split_rows, P(), P())
        + (split_columns, split_columns, split_columns, split_rows),
        out_specs=(split_rows, split_columns, split_columns, split_columns, split_rows),
        check_vma=False,
    )
```

```python
import jax
import jax.numpy as jnp
from jax import lax
from jax.experimental import pallas as pl
from jax.experimental.pallas import tpu as pltpu
from jax.sharding import PartitionSpec as P

LOSS_SCALE = 64.0
BETA_ONE = 0.9
BETA_TWO = 0.95
LEARN_RATE = 0.002
DECAY = 0.1
EPSILON = 1e-08
STEP_COUNT = 20.0

D = 2048
FF = 768
ROWS = 512
FWD_ROWS = 1024
EXPERTS = 32
DEVICES = 128
CAP = 8
SLOTS = DEVICES * CAP
OWN = FF // DEVICES
BLOCK = OWN * D // 8
HALVES = D // 1024
SEND_ONE = FF + D + BLOCK
SEND_TWO = FF + BLOCK
LANES = 256
MIB = 1 << 20

BF16 = jnp.bfloat16
F32 = jnp.float32
I32 = jnp.int32


def iota(shape, dim):
    return lax.broadcasted_iota(I32, shape, dim)


def mm(a, b, dims=((1,), (0,))):
    return lax.dot_general(a, b, (dims, ((), ())), preferred_element_type=F32)


def pick_rows(place_row):
    shape = (SLOTS, DEVICES)
    spread = jnp.where(iota(shape, 0) // 8 == iota(shape, 1), place_row, 0)
    mine = jnp.sum(spread.astype(F32), axis=1, keepdims=True).astype(I32)
    shape = (SLOTS, 8 * EXPERTS)
    row, col = iota(shape, 0), iota(shape, 1)
    hit = (col % EXPERTS == mine) & (col // EXPERTS == row % 8)
    return jnp.where(hit, 1.0, 0.0).astype(BF16)


def pick_columns(place_row):
    shape = (DEVICES, SLOTS)
    wide = jnp.where(iota(shape, 1) // 8 == iota(shape, 0), 1.0, 0.0).astype(BF16)
    mine = mm(place_row.astype(F32).astype(BF16), wide).astype(I32)
    shape = (8 * EXPERTS, SLOTS)
    row, col = iota(shape, 0), iota(shape, 1)
    hit = (row % EXPERTS == mine) & (row // EXPERTS == col % 8)
    return jnp.where(hit, 1.0, 0.0).astype(BF16)


def block_order(to_blocks):
    size = 8 * 8 * OWN
    shape = (size, size)
    blk, mat = (iota(shape, 0), iota(shape, 1)) if to_blocks else (iota(shape, 1), iota(shape, 0))
    target = (blk % 8) * (8 * OWN) + (blk // 8 % 8) * OWN + blk // 64
    return jnp.where(target == mat, 1.0, 0.0).astype(BF16)


def copies(pairs, sems, first=0):
    made = [pltpu.make_async_copy(a, b, sems.at[first + k]) for k, (a, b) in enumerate(pairs)]
    for copy in made:
        copy.start()
    return made


def lanes(k, width=LANES):
    return pl.ds(k * width, width)


NEAR, FAR = pltpu.VMEM, pltpu.HBM


def call(kernel, ins, outs, scratch, mib, flops, moved, name, **more):
    near = pl.BlockSpec(memory_space=NEAR)
    far = pl.BlockSpec(memory_space=pl.ANY)
    run = pl.pallas_call(
        kernel,
        in_specs=[near if space is NEAR else far for _, space in ins],
        out_specs=[near if space is NEAR else far for space, _, _ in outs],
        out_shape=[space(shape, kind) for space, shape, kind in outs],
        scratch_shapes=scratch,
        compiler_params=pltpu.CompilerParams(vmem_limit_bytes=mib * MIB),
        cost_estimate=pl.CostEstimate(flops=flops, bytes_accessed=moved, transcendentals=0),
        name=name,
        **more,
    )
    return run(*[pltpu.with_memory_space_constraint(x, space) for x, space in ins])


def matrix_half(blocks, start, weight, perm, h):
    for pair in range(DEVICES // 16):
        stacked = jnp.concatenate(
            [
                jnp.concatenate(
                    [
                        blocks[pl.ds((pair * 2 + g) * 64, 64), pl.ds(start + (h * OWN + f) * 128, 128)]
                        for g in range(2)
                    ],
                    axis=1,
                )
                for f in range(OWN)
            ],
            axis=0,
        )
        moved = mm(perm, stacked).astype(BF16)
        for g in range(2):
            for s in range(8):
                weight[pl.ds((pair * 2 + g) * 8 * OWN, 8 * OWN), pl.ds((h * 8 + s) * 128, 128)] = moved[
                    s * 8 * OWN : (s + 1) * 8 * OWN, g * 128 : (g + 1) * 128
                ]


def blocks_half(matrix, blocks, perm, h, done):
    for pair in range(DEVICES // 16):
        stacked = jnp.concatenate(
            [
                jnp.concatenate(
                    [
                        matrix[pl.ds((pair * 2 + g) * 8 * OWN, 8 * OWN), pl.ds((h * 8 + s) * 128, 128)]
                        for g in range(2)
                    ],
                    axis=1,
                )
                for s in range(8)
            ],
            axis=0,
        )
        moved = mm(perm, stacked).astype(BF16)
        for g in range(2):
            for f in range(OWN):
                blocks[pl.ds((pair * 2 + g) * 64, 64), pl.ds((h * OWN + f) * 128, 128)] = moved[
                    f * 64 : (f + 1) * 64, g * 128 : (g + 1) * 128
                ]
        done(pair)


def interleave(inner, outer, back):
    shape = (inner * outer, inner * outer)
    a, b = (iota(shape, 1), iota(shape, 0)) if back else (iota(shape, 0), iota(shape, 1))
    return jnp.where(a % outer * inner + a // outer == b, 1.0, 0.0).astype(BF16)


def stacked_master(block):
    return jnp.concatenate(
        [
            jnp.concatenate(
                [block[:, (h * 8 + s) * 128 : (h * 8 + s + 1) * 128] for h in range(HALVES)], axis=1
            )
            for s in range(8)
        ],
        axis=0,
    )


def dispatch_kernel(
    route, place, saved, grad, master, send, position, route_v, place_v, saved_v, grad_v, master_v, position_v, sems
):
    got_route, got_place, got_saved, got_grad, got_master = copies(
        [(route, route_v), (place, place_v), (saved, saved_v), (grad, grad_v), (master, master_v)], sems
    )
    got_route.wait()
    target = route_v[...]
    ones = jnp.where(iota((DEVICES, ROWS), 0) == target, 1.0, 0.0)
    shape = (ROWS, ROWS)
    upto = jnp.where(iota(shape, 0) < iota(shape, 1), 1.0, 0.0).astype(BF16)
    earlier = mm(ones.astype(BF16), upto)
    rank = jnp.sum(ones * earlier, axis=0, keepdims=True).astype(I32)
    where = target * CAP + rank
    position_v[...] = where
    (told,) = copies([(position_v, position)], sems, 5)
    slot_of = jnp.where(iota((SLOTS, ROWS), 0) == where, 1.0, 0.0).astype(BF16)
    got_saved.wait()
    send[:, pl.ds(0, FF)] = mm(slot_of, saved_v[...]).astype(BF16)
    got_grad.wait()
    for k in range(2):
        tall = slice(k * SLOTS // 2, (k + 1) * SLOTS // 2)
        send[tall, pl.ds(FF, D)] = mm(slot_of[tall], grad_v[...]).astype(BF16)
    got_place.wait()
    got_master.wait()
    pick = pick_rows(place_v[...])
    for f in range(OWN):
        rows = stacked_master(master_v[:, lanes(f, D)]).astype(BF16)
        picked = mm(pick, rows).astype(BF16)
        for h in range(HALVES):
            send[:, lanes(22 + h * OWN + f, 128)] = picked[:, h * 128 : (h + 1) * 128]
    told.wait()


def dispatch(route, place, saved, grad, master):
    return call(
        dispatch_kernel,
        [(route, FAR), (place, FAR), (saved, FAR), (grad, FAR), (master, FAR)],
        [(NEAR, (SLOTS, SEND_ONE), BF16), (FAR, (1, ROWS), I32)],
        [
            pltpu.VMEM((1, ROWS), I32),
            pltpu.VMEM((1, DEVICES), I32),
            pltpu.VMEM((ROWS, FF), BF16),
            pltpu.VMEM((ROWS, D), BF16),
            pltpu.VMEM((EXPERTS, OWN * D), F32),
            pltpu.VMEM((1, ROWS), I32),
            pltpu.SemaphoreType.DMA((6,)),
        ],
        16,
        4_000_000_000,
        14_000_000,
        "dispatch_rows",
    )


def partial_kernel(got, out, part_v, out_v, sems):
    perm = block_order(True)
    left = got[:, pl.ds(0, FF)].T
    sent = []
    for h in range(HALVES):
        for m in range(2):
            tall = slice(m * FF // 2, (m + 1) * FF // 2)
            wide = mm(left[tall], got[:, pl.ds(FF + h * 1024, 1024)])
            part_v[tall, lanes(h, 1024)] = (wide * (1.0 / LOSS_SCALE)).astype(BF16)

        def ship(pair, h=h):
            if pair % 2:
                at = (lanes(pair // 2), lanes(h, BLOCK // HALVES))
                sent.extend(copies([(out_v.at[at], out.at[at])], sems, 4 * h + pair // 2))

        blocks_half(part_v, out_v, perm, h, ship)
    for copy in sent:
        copy.wait()


def partials(got):
    return call(
        partial_kernel,
        [(got, NEAR)],
        [(FAR, (SLOTS, BLOCK), BF16)],
        [
            pltpu.VMEM((FF, D), BF16),
            pltpu.VMEM((SLOTS, BLOCK), BF16),
            pltpu.SemaphoreType.DMA((4 * HALVES,)),
        ],
        20,
        4_400_000_000,
        9_000_000,
        "partial_blocks",
    )[0]


def input_kernel(
    position, rows, got, out, back, ordered, position_v, rows_v, weight, out_v, back_v, ordered_v, sems
):
    got_position, got_rows = copies([(position, position_v), (rows, rows_v)], sems)
    perm = block_order(False)
    for h in range(HALVES):
        matrix_half(got, FF + D, weight, perm, h)
    sent = []
    for k in range(4):
        tall = pl.ds(k * 256, 256)
        out_v[tall, :] = mm(got[tall, pl.ds(FF, D)], weight[...], ((1,), (1,))).astype(BF16)
        sent += copies([(out_v.at[tall, :], out.at[tall, :])], sems, 2 + k)
    got_position.wait()
    shape = (ROWS, ROWS)
    spread = jnp.where(iota(shape, 0) == iota(shape, 1), position_v[...], 0)
    where = jnp.sum(spread.astype(F32), axis=1, keepdims=True).astype(I32)
    back_v[...] = jnp.where(iota((ROWS, SLOTS), 1) == where, 1.0, 0.0).astype(BF16)
    sent += copies([(back_v, back)], sems, 6)
    got_rows.wait()
    shape = (FF, FF)
    natural, target = iota(shape, 0), iota(shape, 1)
    order = jnp.where(target % DEVICES * OWN + target // DEVICES == natural, 1.0, 0.0).astype(BF16)
    ordered_v[...] = mm(rows_v[...], order).astype(BF16)
    sent += copies([(ordered_v, ordered)], sems, 7)
    for copy in sent:
        copy.wait()


def input_parts(got, position, rows):
    return call(
        input_kernel,
        [(position, FAR), (rows, FAR), (got, NEAR)],
        [(FAR, (SLOTS, FF), BF16), (FAR, (ROWS, SLOTS), BF16), (FAR, rows.shape, BF16)],
        [
            pltpu.VMEM((1, ROWS), I32),
            pltpu.VMEM((FWD_ROWS, FF), BF16),
            pltpu.VMEM((FF, D), BF16),
            pltpu.VMEM((SLOTS, FF), BF16),
            pltpu.VMEM((ROWS, SLOTS), BF16),
            pltpu.VMEM((FWD_ROWS, FF), BF16),
            pltpu.SemaphoreType.DMA((8,)),
        ],
        20,
        4_400_000_000,
        12_000_000,
        "input_parts",
    )


def adam_kernel(
    place_now, place_next, arrived, returning, master, one, two, send, new_master, new_one, new_two,
    now_v, then_v, master_v, one_v, two_v, total_v, rows_v, place_sems, in_sems,
):
    got_now, got_then = copies([(place_now, now_v), (place_next, then_v)], place_sems)
    landed = []
    for part in range(1):
        at = lanes(part, OWN // 1 * D)
        landed += copies(
            [(a.at[:, at], b.at[:, at]) for a, b in ((master, master_v), (one, one_v), (two, two_v))], in_sems, 3 * part
        )
    (merged,) = copies([(returning, send.at[:, pl.ds(0, FF)])], place_sems, 2)
    got_now.wait()
    total_v[...] = mm(pick_columns(now_v[...]), arrived[...])
    for f in range(OWN):
        if f % 6 == 0:
            for copy in landed[f // 6 * 3 : f // 6 * 3 + 3]:
                copy.wait()
        for h in range(HALVES):
            mine = lanes(h * OWN + f, 128)
            for s in range(8):
                owned = pl.ds(s * EXPERTS, EXPERTS)
                at = pl.ds(f * D + (h * 8 + s) * 128, 128)
                gradient = total_v[owned, mine]
                weight = master_v[:, at]
                first = BETA_ONE * one_v[:, at] + (1.0 - BETA_ONE) * gradient
                second = BETA_TWO * two_v[:, at] + (1.0 - BETA_TWO) * gradient * gradient
                second_hat = second * (1.0 / (1.0 - BETA_TWO**STEP_COUNT))
                root = second_hat * lax.rsqrt(second_hat)
                step = first * (LEARN_RATE / (1.0 - BETA_ONE**STEP_COUNT)) / (root + EPSILON)
                updated = weight * (1.0 - LEARN_RATE * DECAY) - step
                new_one[:, at] = first
                new_two[:, at] = second
                new_master[:, at] = updated
                rows_v[owned, mine] = updated.astype(BF16)
    got_then.wait()
    send[:, pl.ds(FF, BLOCK)] = mm(pick_rows(then_v[...]), rows_v[...]).astype(BF16)
    merged.wait()


def adam(place_now, place_next, arrived, returning, master, one, two):
    state = (NEAR, master.shape, F32)
    flat = pltpu.VMEM((EXPERTS, OWN * D), F32)
    return call(
        adam_kernel,
        [(x, NEAR if x is arrived else FAR) for x in (place_now, place_next, arrived, returning, master, one, two)],
        [(NEAR, (SLOTS, SEND_TWO), BF16), state, state, state],
        [pltpu.VMEM((1, DEVICES), I32)] * 2
        + [flat] * 3
        + [pltpu.VMEM((8 * EXPERTS, BLOCK), F32), pltpu.VMEM((8 * EXPERTS, BLOCK), BF16)]
        + [pltpu.SemaphoreType.DMA((3,))]
        + [pltpu.SemaphoreType.DMA((3,))],
        16,
        1_700_000_000,
        16_000_000,
        "adam_step",
    )


def ordered_half(blocks, start, weight, perm, h):
    for g in range(DEVICES // 16):
        moved = mm(perm, blocks[pl.ds(g * 128, 128), pl.ds(start + h * OWN * 128, OWN * 128)]).astype(BF16)
        for s in range(8):
            for f in range(OWN):
                weight[pl.ds(f * DEVICES + g * 16, 16), pl.ds((h * 8 + s) * 128, 128)] = moved[
                    s * 16 : (s + 1) * 16, f * 128 : (f + 1) * 128
                ]


def forward_kernel(
    landed, back, rows, master, one, two, out, input_grad, new_master, new_one, new_two, weight, out_v, grad_v, sems
):
    kept = copies([(master, new_master), (one, new_one), (two, new_two)], sems, 9)
    perm = interleave(8, 16, False)
    for h in range(HALVES):
        ordered_half(landed, FF, weight, perm, h)
    grad_v[...] = mm(back[...], landed[:, pl.ds(0, FF)]).astype(BF16)
    sent = copies([(grad_v, input_grad)], sems)
    for k in range(8):
        tall = lanes(k, FWD_ROWS // 8)
        out_v[tall, :] = mm(rows[tall, :], weight[...]).astype(BF16)
        sent += copies([(out_v.at[tall, :], out.at[tall, :])], sems, 1 + k)
    for copy in kept + sent:
        copy.wait()


def forward(landed, back, rows, *states):
    return call(
        forward_kernel,
        [(x, NEAR) for x in (landed, back, rows) + states],
        [(FAR, (FWD_ROWS, D), BF16), (FAR, (ROWS, FF), BF16)] + [(FAR, x.shape, F32) for x in states],
        [
            pltpu.VMEM((FF, D), BF16),
            pltpu.VMEM((FWD_ROWS, D), BF16),
            pltpu.VMEM((ROWS, FF), BF16),
            pltpu.SemaphoreType.DMA((12,)),
        ],
        24,
        5_200_000_000,
        13_000_000,
        "forward_rows",
    )


def exchange(blocks):
    split = blocks.reshape(DEVICES, 8, blocks.shape[1])
    moved = lax.all_to_all(split, ("expert", "opt"), split_axis=0, concat_axis=0, tiled=True)
    return moved.reshape(blocks.shape)


def per_device(out_grad, saved_input, route, place_now, place_next, master, moment_one, moment_two, fwd_input):
    now, then = place_now.reshape(1, DEVICES), place_next.reshape(1, DEVICES)
    send, position = dispatch(route.reshape(1, ROWS), now, saved_input, out_grad, master)
    got = exchange(send)
    arrived = exchange(partials(got))
    returning, back, rows = input_parts(got, position, fwd_input)
    sending, *states = adam(now, then, arrived, returning, master, moment_one, moment_two)
    landed = exchange(sending)
    fwd_output, input_grad, new_master, new_one, new_two = forward(landed, back, rows, *states)
    return (input_grad, new_master, new_one, new_two, fwd_output)


def solution(mesh):
    split_rows = P(("expert", "opt"), None)
    split_columns = P(None, ("expert", "opt"))
    return jax.shard_map(
        per_device,
        mesh=mesh,
        in_specs=(split_rows, split_rows, split_rows, P(), P())
        + (split_columns, split_columns, split_columns, split_rows),
        out_specs=(split_rows, split_columns, split_columns, split_columns, split_rows),
        check_vma=False,
    )
```

```python
import jax
import jax.numpy as jnp
from jax import lax
from jax.experimental import pallas as pl
from jax.experimental.pallas import tpu as pltpu
from jax.sharding import PartitionSpec as P

LOSS_SCALE = 64.0
BETA_ONE = 0.9
BETA_TWO = 0.95
LEARN_RATE = 0.002
DECAY = 0.1
EPSILON = 1e-08
STEP_COUNT = 20.0

D = 2048
FF = 768
ROWS = 512
FWD_ROWS = 1024
EXPERTS = 32
DEVICES = 128
CAP = 8
SLOTS = DEVICES * CAP
OWN = FF // DEVICES
BLOCK = OWN * D // 8
HALVES = D // 1024
SEND_ONE = FF + D + BLOCK
SEND_TWO = FF + BLOCK
LANES = 256
MIB = 1 << 20

BF16 = jnp.bfloat16
F32 = jnp.float32
I32 = jnp.int32


def iota(shape, dim):
    return lax.broadcasted_iota(I32, shape, dim)


def mm(a, b, dims=((1,), (0,))):
    return lax.dot_general(a, b, (dims, ((), ())), preferred_element_type=F32)


def pick_rows(place_row):
    shape = (SLOTS, DEVICES)
    spread = jnp.where(iota(shape, 0) // 8 == iota(shape, 1), place_row, 0)
    mine = jnp.sum(spread.astype(F32), axis=1, keepdims=True).astype(I32)
    shape = (SLOTS, 8 * EXPERTS)
    row, col = iota(shape, 0), iota(shape, 1)
    hit = (col % EXPERTS == mine) & (col // EXPERTS == row % 8)
    return jnp.where(hit, 1.0, 0.0).astype(BF16)


def pick_columns(place_row):
    shape = (DEVICES, SLOTS)
    wide = jnp.where(iota(shape, 1) // 8 == iota(shape, 0), 1.0, 0.0).astype(BF16)
    mine = mm(place_row.astype(F32).astype(BF16), wide).astype(I32)
    shape = (8 * EXPERTS, SLOTS)
    row, col = iota(shape, 0), iota(shape, 1)
    hit = (row % EXPERTS == mine) & (row // EXPERTS == col % 8)
    return jnp.where(hit, 1.0, 0.0).astype(BF16)


def block_order(to_blocks):
    size = 8 * 8 * OWN
    shape = (size, size)
    blk, mat = (iota(shape, 0), iota(shape, 1)) if to_blocks else (iota(shape, 1), iota(shape, 0))
    target = (blk % 8) * (8 * OWN) + (blk // 8 % 8) * OWN + blk // 64
    return jnp.where(target == mat, 1.0, 0.0).astype(BF16)


def copies(pairs, sems, first=0):
    made = [pltpu.make_async_copy(a, b, sems.at[first + k]) for k, (a, b) in enumerate(pairs)]
    for copy in made:
        copy.start()
    return made


def lanes(k, width=LANES):
    return pl.ds(k * width, width)


NEAR, FAR = pltpu.VMEM, pltpu.HBM


def call(kernel, ins, outs, scratch, mib, flops, moved, name, **more):
    near = pl.BlockSpec(memory_space=NEAR)
    far = pl.BlockSpec(memory_space=pl.ANY)
    run = pl.pallas_call(
        kernel,
        in_specs=[near if space is NEAR else far for _, space in ins],
        out_specs=[near if space is NEAR else far for space, _, _ in outs],
        out_shape=[space(shape, kind) for space, shape, kind in outs],
        scratch_shapes=scratch,
        compiler_params=pltpu.CompilerParams(vmem_limit_bytes=mib * MIB),
        cost_estimate=pl.CostEstimate(flops=flops, bytes_accessed=moved, transcendentals=0),
        name=name,
        **more,
    )
    return run(*[pltpu.with_memory_space_constraint(x, space) for x, space in ins])


def matrix_half(blocks, start, weight, perm, h):
    for pair in range(DEVICES // 16):
        stacked = jnp.concatenate(
            [
                jnp.concatenate(
                    [
                        blocks[pl.ds((pair * 2 + g) * 64, 64), pl.ds(start + (h * OWN + f) * 128, 128)]
                        for g in range(2)
                    ],
                    axis=1,
                )
                for f in range(OWN)
            ],
            axis=0,
        )
        moved = mm(perm, stacked).astype(BF16)
        for g in range(2):
            for s in range(8):
                weight[pl.ds((pair * 2 + g) * 8 * OWN, 8 * OWN), pl.ds((h * 8 + s) * 128, 128)] = moved[
                    s * 8 * OWN : (s + 1) * 8 * OWN, g * 128 : (g + 1) * 128
                ]


def blocks_half(matrix, blocks, perm, h, done):
    for pair in range(DEVICES // 16):
        stacked = jnp.concatenate(
            [
                jnp.concatenate(
                    [
                        matrix[pl.ds((pair * 2 + g) * 8 * OWN, 8 * OWN), pl.ds((h * 8 + s) * 128, 128)]
                        for g in range(2)
                    ],
                    axis=1,
                )
                for s in range(8)
            ],
            axis=0,
        )
        moved = mm(perm, stacked).astype(BF16)
        for g in range(2):
            for f in range(OWN):
                blocks[pl.ds((pair * 2 + g) * 64, 64), pl.ds((h * OWN + f) * 128, 128)] = moved[
                    f * 64 : (f + 1) * 64, g * 128 : (g + 1) * 128
                ]
        done(pair)


def interleave(inner, outer, back):
    shape = (inner * outer, inner * outer)
    a, b = (iota(shape, 1), iota(shape, 0)) if back else (iota(shape, 0), iota(shape, 1))
    return jnp.where(a % outer * inner + a // outer == b, 1.0, 0.0).astype(BF16)


def stacked_master(block):
    return jnp.concatenate(
        [
            jnp.concatenate(
                [block[:, (h * 8 + s) * 128 : (h * 8 + s + 1) * 128] for h in range(HALVES)], axis=1
            )
            for s in range(8)
        ],
        axis=0,
    )


def dispatch_kernel(
    route, place, saved, grad, master, send, position, route_v, place_v, saved_v, grad_v, master_v, position_v, sems
):
    got_route, got_place, got_saved, got_grad, got_master = copies(
        [(route, route_v), (place, place_v), (saved, saved_v), (grad, grad_v), (master, master_v)], sems
    )
    got_route.wait()
    target = route_v[...]
    ones = jnp.where(iota((DEVICES, ROWS), 0) == target, 1.0, 0.0)
    shape = (ROWS, ROWS)
    upto = jnp.where(iota(shape, 0) < iota(shape, 1), 1.0, 0.0).astype(BF16)
    earlier = mm(ones.astype(BF16), upto)
    rank = jnp.sum(ones * earlier, axis=0, keepdims=True).astype(I32)
    where = target * CAP + rank
    position_v[...] = where
    (told,) = copies([(position_v, position)], sems, 5)
    slot_of = jnp.where(iota((SLOTS, ROWS), 0) == where, 1.0, 0.0).astype(BF16)
    got_saved.wait()
    send[:, pl.ds(0, FF)] = mm(slot_of, saved_v[...]).astype(BF16)
    got_grad.wait()
    for k in range(2):
        tall = slice(k * SLOTS // 2, (k + 1) * SLOTS // 2)
        send[tall, pl.ds(FF, D)] = mm(slot_of[tall], grad_v[...]).astype(BF16)
    got_place.wait()
    got_master.wait()
    pick = pick_rows(place_v[...])
    for f in range(OWN):
        rows = stacked_master(master_v[:, lanes(f, D)]).astype(BF16)
        picked = mm(pick, rows).astype(BF16)
        for h in range(HALVES):
            send[:, lanes(22 + h * OWN + f, 128)] = picked[:, h * 128 : (h + 1) * 128]
    told.wait()


def dispatch(route, place, saved, grad, master):
    return call(
        dispatch_kernel,
        [(route, FAR), (place, FAR), (saved, FAR), (grad, FAR), (master, FAR)],
        [(NEAR, (SLOTS, SEND_ONE), BF16), (FAR, (1, ROWS), I32)],
        [
            pltpu.VMEM((1, ROWS), I32),
            pltpu.VMEM((1, DEVICES), I32),
            pltpu.VMEM((ROWS, FF), BF16),
            pltpu.VMEM((ROWS, D), BF16),
            pltpu.VMEM((EXPERTS, OWN * D), F32),
            pltpu.VMEM((1, ROWS), I32),
            pltpu.SemaphoreType.DMA((6,)),
        ],
        16,
        4_000_000_000,
        14_000_000,
        "dispatch_rows",
    )


def partial_kernel(got, out, part_v, out_v, sems):
    perm = block_order(True)
    left = got[:, pl.ds(0, FF)].T
    sent = []
    for h in range(HALVES):
        for m in range(2):
            tall = slice(m * FF // 2, (m + 1) * FF // 2)
            wide = mm(left[tall], got[:, pl.ds(FF + h * 1024, 1024)])
            part_v[tall, lanes(h, 1024)] = (wide * (1.0 / LOSS_SCALE)).astype(BF16)

        def ship(pair, h=h):
            if pair % 2:
                at = (lanes(pair // 2), lanes(h, BLOCK // HALVES))
                sent.extend(copies([(out_v.at[at], out.at[at])], sems, 4 * h + pair // 2))

        blocks_half(part_v, out_v, perm, h, ship)
    for copy in sent:
        copy.wait()


def partials(got):
    return call(
        partial_kernel,
        [(got, NEAR)],
        [(FAR, (SLOTS, BLOCK), BF16)],
        [
            pltpu.VMEM((FF, D), BF16),
            pltpu.VMEM((SLOTS, BLOCK), BF16),
            pltpu.SemaphoreType.DMA((4 * HALVES,)),
        ],
        20,
        4_400_000_000,
        9_000_000,
        "partial_blocks",
    )[0]


def input_kernel(
    position, rows, got, out, back, ordered, position_v, rows_v, weight, out_v, back_v, ordered_v, sems
):
    got_position, got_rows = copies([(position, position_v), (rows, rows_v)], sems)
    perm = block_order(False)
    for h in range(HALVES):
        matrix_half(got, FF + D, weight, perm, h)
    sent = []
    for k in range(4):
        tall = pl.ds(k * 256, 256)
        out_v[tall, :] = mm(got[tall, pl.ds(FF, D)], weight[...], ((1,), (1,))).astype(BF16)
        sent += copies([(out_v.at[tall, :], out.at[tall, :])], sems, 2 + k)
    got_position.wait()
    shape = (ROWS, ROWS)
    spread = jnp.where(iota(shape, 0) == iota(shape, 1), position_v[...], 0)
    where = jnp.sum(spread.astype(F32), axis=1, keepdims=True).astype(I32)
    back_v[...] = jnp.where(iota((ROWS, SLOTS), 1) == where, 1.0, 0.0).astype(BF16)
    sent += copies([(back_v, back)], sems, 6)
    got_rows.wait()
    shape = (FF, FF)
    natural, target = iota(shape, 0), iota(shape, 1)
    order = jnp.where(target % DEVICES * OWN + target // DEVICES == natural, 1.0, 0.0).astype(BF16)
    ordered_v[...] = mm(rows_v[...], order).astype(BF16)
    sent += copies([(ordered_v, ordered)], sems, 7)
    for copy in sent:
        copy.wait()


def input_parts(got, position, rows):
    return call(
        input_kernel,
        [(position, FAR), (rows, FAR), (got, NEAR)],
        [(FAR, (SLOTS, FF), BF16), (FAR, (ROWS, SLOTS), BF16), (FAR, rows.shape, BF16)],
        [
            pltpu.VMEM((1, ROWS), I32),
            pltpu.VMEM((FWD_ROWS, FF), BF16),
            pltpu.VMEM((FF, D), BF16),
            pltpu.VMEM((SLOTS, FF), BF16),
            pltpu.VMEM((ROWS, SLOTS), BF16),
            pltpu.VMEM((FWD_ROWS, FF), BF16),
            pltpu.SemaphoreType.DMA((8,)),
        ],
        20,
        4_400_000_000,
        12_000_000,
        "input_parts",
    )


def adam_kernel(
    place_now, place_next, arrived, returning, master, one, two, send, new_master, new_one, new_two,
    now_v, then_v, master_v, one_v, two_v, total_v, rows_v, place_sems, in_sems,
):
    got_now, got_then = copies([(place_now, now_v), (place_next, then_v)], place_sems)
    landed = []
    for part in range(1):
        at = lanes(part, OWN // 1 * D)
        landed += copies(
            [(a.at[:, at], b.at[:, at]) for a, b in ((master, master_v), (one, one_v), (two, two_v))], in_sems, 3 * part
        )
    (merged,) = copies([(returning, send.at[:, pl.ds(0, FF)])], place_sems, 2)
    got_now.wait()
    total_v[...] = mm(pick_columns(now_v[...]), arrived[...])
    for f in range(OWN):
        if f % 6 == 0:
            for copy in landed[f // 6 * 3 : f // 6 * 3 + 3]:
                copy.wait()
        for h in range(HALVES):
            mine = lanes(h * OWN + f, 128)
            for s in range(8):
                owned = pl.ds(s * EXPERTS, EXPERTS)
                at = pl.ds(f * D + (h * 8 + s) * 128, 128)
                gradient = total_v[owned, mine]
                weight = master_v[:, at]
                first = BETA_ONE * one_v[:, at] + (1.0 - BETA_ONE) * gradient
                second = BETA_TWO * two_v[:, at] + (1.0 - BETA_TWO) * gradient * gradient
                second_hat = second * (1.0 / (1.0 - BETA_TWO**STEP_COUNT))
                root = second_hat * lax.rsqrt(second_hat)
                step = first * (LEARN_RATE / (1.0 - BETA_ONE**STEP_COUNT)) / (root + EPSILON)
                updated = weight * (1.0 - LEARN_RATE * DECAY) - step
                new_one[:, at] = first
                new_two[:, at] = second
                new_master[:, at] = updated
                rows_v[owned, mine] = updated.astype(BF16)
    got_then.wait()
    send[:, pl.ds(FF, BLOCK)] = mm(pick_rows(then_v[...]), rows_v[...]).astype(BF16)
    merged.wait()


def adam(place_now, place_next, arrived, returning, master, one, two):
    state = (NEAR, master.shape, F32)
    flat = pltpu.VMEM((EXPERTS, OWN * D), F32)
    return call(
        adam_kernel,
        [(x, NEAR if x is arrived else FAR) for x in (place_now, place_next, arrived, returning, master, one, two)],
        [(NEAR, (SLOTS, SEND_TWO), BF16), state, state, state],
        [pltpu.VMEM((1, DEVICES), I32)] * 2
        + [flat] * 3
        + [pltpu.VMEM((8 * EXPERTS, BLOCK), F32), pltpu.VMEM((8 * EXPERTS, BLOCK), BF16)]
        + [pltpu.SemaphoreType.DMA((3,))]
        + [pltpu.SemaphoreType.DMA((3,))],
        16,
        1_700_000_000,
        16_000_000,
        "adam_step",
    )


def ordered_half(blocks, start, weight, perm, h):
    for g in range(DEVICES // 16):
        moved = mm(perm, blocks[pl.ds(g * 128, 128), pl.ds(start + h * OWN * 128, OWN * 128)]).astype(BF16)
        for s in range(8):
            for f in range(OWN):
                weight[pl.ds(f * DEVICES + g * 16, 16), pl.ds((h * 8 + s) * 128, 128)] = moved[
                    s * 16 : (s + 1) * 16, f * 128 : (f + 1) * 128
                ]


def forward_kernel(
    landed, back, rows, master, one, two, out, input_grad, new_master, new_one, new_two, weight, out_v, grad_v, sems
):
    kept = copies([(master, new_master), (one, new_one), (two, new_two)], sems, 9)
    perm = interleave(8, 16, False)
    for h in range(HALVES):
        ordered_half(landed, FF, weight, perm, h)
    grad_v[...] = mm(back[...], landed[:, pl.ds(0, FF)]).astype(BF16)
    sent = copies([(grad_v, input_grad)], sems)
    first = 0
    for k, size in enumerate((320, 320, 256, 128)):
        tall = pl.ds(first, size)
        first += size
        out_v[tall, :] = mm(rows[tall, :], weight[...]).astype(BF16)
        sent += copies([(out_v.at[tall, :], out.at[tall, :])], sems, 1 + k)
    for copy in kept + sent:
        copy.wait()


def forward(landed, back, rows, *states):
    return call(
        forward_kernel,
        [(x, NEAR) for x in (landed, back, rows) + states],
        [(FAR, (FWD_ROWS, D), BF16), (FAR, (ROWS, FF), BF16)] + [(FAR, x.shape, F32) for x in states],
        [
            pltpu.VMEM((FF, D), BF16),
            pltpu.VMEM((FWD_ROWS, D), BF16),
            pltpu.VMEM((ROWS, FF), BF16),
            pltpu.SemaphoreType.DMA((12,)),
        ],
        24,
        5_200_000_000,
        13_000_000,
        "forward_rows",
    )


def exchange(blocks):
    split = blocks.reshape(DEVICES, 8, blocks.shape[1])
    moved = lax.all_to_all(split, ("expert", "opt"), split_axis=0, concat_axis=0, tiled=True)
    return moved.reshape(blocks.shape)


def per_device(out_grad, saved_input, route, place_now, place_next, master, moment_one, moment_two, fwd_input):
    now, then = place_now.reshape(1, DEVICES), place_next.reshape(1, DEVICES)
    send, position = dispatch(route.reshape(1, ROWS), now, saved_input, out_grad, master)
    got = exchange(send)
    arrived = exchange(partials(got))
    returning, back, rows = input_parts(got, position, fwd_input)
    sending, *states = adam(now, then, arrived, returning, master, moment_one, moment_two)
    landed = exchange(sending)
    fwd_output, input_grad, new_master, new_one, new_two = forward(landed, back, rows, *states)
    return (input_grad, new_master, new_one, new_two, fwd_output)


def solution(mesh):
    split_rows = P(("expert", "opt"), None)
    split_columns = P(None, ("expert", "opt"))
    return jax.shard_map(
        per_device,
        mesh=mesh,
        in_specs=(split_rows, split_rows, split_rows, P(), P())
        + (split_columns, split_columns, split_columns, split_rows),
        out_specs=(split_rows, split_columns, split_columns, split_columns, split_rows),
        check_vma=False,
    )
```
